128 devices in a mesh: rows: 16 (over y, x), cols: 8 (over z, core).
Axes of the slice: x: 4, y: 4, z: 4, core: 2. Of those that a mesh axis runs over, the one named last changes fastest.
Arguments:
- embeddings: bfloat16 [12288, 1024], P('rows'), may hold values from -6 to 6
- landmarks: bfloat16 [8192, 1024], P('cols', 'rows'), may hold values from -6 to 6
- factor_rows: bfloat16 [8192, 16, 512], P('cols', None, 'rows'), may hold values from -0.0625 to 0.0625
- diag_inverse: bfloat16 [16, 512, 512], P('cols'), as said below
Outputs:
- features: bfloat16 [12288, 8192], P('rows', 'cols')
The draws below stay inside these ranges and needn't reach their ends.
Inputs may be any that keep to these rules, and one draw needn't show every extreme that they name: `diag_inverse`: each block is lower triangular with a positive diagonal.
All inputs are finite; a program needn't handle non-finite values.
Results may differ from the reference program's by a relative error of at most 0.011.
Values may be sent and summed in bfloat16 or wider, within the bound.
No kernel may reach another device: no remote copies, remote signals or barrier semaphores. Data moves between devices by JAX's collectives and lax.ppermute only.
A program may use at most 128 MiB of HBM per device.

```python
import math
import jax
import jax.numpy as jnp
from jax import lax

D = 1024
B = 512
NB = 16
LANDMARKS = 8192
TOKENS = 12288


def draw_embeddings(key, part):
    key = jax.random.fold_in(key, 11)
    values = jnp.clip(jax.random.normal(key, (TOKENS, D), jnp.float32), -6.0, 6.0)
    return values.astype(jnp.bfloat16)


def draw_landmarks(key, part):
    key = jax.random.fold_in(key, 12)
    values = jnp.clip(jax.random.normal(key, (LANDMARKS, D), jnp.float32), -6.0, 6.0)
    return values.astype(jnp.bfloat16)


def draw_diag_inverse(key, part):
    key = jax.random.fold_in(key, 13)
    key_diag, key_lower = jax.random.split(key)
    spread = math.sqrt(0.5 / B)
    diagonal = jax.random.uniform(key_diag, (NB, B, B), jnp.float32, 0.8, 1.25)
    lower = jnp.clip(jax.random.normal(key_lower, (NB, B, B), jnp.float32), -6.0, 6.0) * spread
    row_place = lax.broadcasted_iota(jnp.int32, (NB, B, B), 1)
    col_place = lax.broadcasted_iota(jnp.int32, (NB, B, B), 2)
    result = jnp.where(row_place > col_place, lower, 0.0) + jnp.where(row_place == col_place, diagonal, 0.0)
    return result.astype(jnp.bfloat16)


def level_of(stream_key, shape, cuts, low, largest):
    loudness = 1.0
    for axis_at, parts in cuts:
        heights = jax.random.uniform(jax.random.fold_in(jax.random.fold_in(stream_key, 6), axis_at), (parts,), jnp.float32, low / len(cuts), largest / len(cuts))
        loudness = loudness * jnp.repeat(jnp.exp(heights), shape[axis_at] // parts).reshape((-1,) + (1,) * (len(shape) - 1 - axis_at))
    return loudness


def noise(own_key, dims, scale, limit, pieces=(), kind=jnp.bfloat16):
    factor_of = level_of(own_key, dims, pieces, -0.22, 0.18) if pieces else 1.0
    values = jax.random.normal(own_key, dims, jnp.float32) * scale * factor_of
    return jnp.minimum(jnp.maximum(values, -limit), limit).astype(kind)


def setup_inputs(seed: int = 0) -> dict:
    key_of = jax.random.split(jax.random.key(seed), 5)
    embeddings = draw_embeddings(jax.random.fold_in(key_of[4], 71), 0)
    landmarks = draw_landmarks(jax.random.fold_in(key_of[4], 71), 0)
    factor_rows = noise(key_of[2], (LANDMARKS, NB, B), (B * NB) ** -0.5, 0.0625, ((0, 8), (2, 16)))
    diag_inverse = draw_diag_inverse(jax.random.fold_in(key_of[4], 71), 0)
    return {"embeddings": embeddings, "landmarks": landmarks, "factor_rows": factor_rows, "diag_inverse": diag_inverse}


def reference(embeddings, landmarks, factor_rows, diag_inverse):
    scale = 0.5 / math.sqrt(D)
    solved_list = []
    for block in range(NB):
        points = landmarks[block * B:(block + 1) * B]
        scores = jnp.dot(embeddings, points.T, preferred_element_type=jnp.float32)
        current = jnp.exp(scores * scale)
        if block > 0:
            earlier = jnp.concatenate(solved_list, axis=1)
            factor_block = factor_rows[block * B:(block + 1) * B, :block, :].reshape(B, block * B)
            current = current - jnp.dot(earlier, factor_block.T, preferred_element_type=jnp.float32)
        rounded = current.astype(jnp.bfloat16)
        product = jnp.dot(rounded, diag_inverse[block].T, preferred_element_type=jnp.float32)
        solved_list.append(product.astype(jnp.bfloat16))
    return jnp.concatenate(solved_list, axis=1)
```

```python
import functools
import math

import jax
import jax.numpy as jnp
from jax import lax
from jax.experimental import pallas as pl
from jax.experimental.pallas import tpu as pltpu
from jax.sharding import PartitionSpec as P

CHUNKS = 2
BF = jnp.bfloat16
F32 = jnp.float32


def mm(a, b):
    return jnp.dot(a, b, preferred_element_type=F32)


def scores_kernel(scale, info, emb, lm_own, lm_oth, out):
    core = info[1]
    depth = emb.shape[1]
    width = lm_own.shape[2]
    for slot, lm in ((core, lm_own), (1 - core, lm_oth)):
        points = lm[...].reshape(depth, width)
        out[0, pl.ds(slot, 1)] = jnp.exp(mm(emb[...], points) * scale)[None]


def solve(running, even, odd, dt_even, dt_odd, store):
    size = dt_even.shape[1]
    r0, r1, r2, r3 = (running[i // 2, :, (i % 2) * size:(i % 2 + 1) * size] for i in range(4))
    l10 = even[:, 0:32, 0:size].reshape(size, size)
    l32 = even[:, 0:32, size:].reshape(size, size)
    l20 = odd[:, 0:32, 0:size].reshape(size, size)
    l30 = odd[:, 0:32, size:].reshape(size, size)
    l21 = odd[:, 32:64, 0:size].reshape(size, size)
    l31 = odd[:, 32:64, size:].reshape(size, size)
    f0 = mm(r0.astype(BF), dt_even[0]).astype(BF)
    store(0, f0)
    r1 = r1 - mm(f0, l10)
    f1 = mm(r1.astype(BF), dt_even[1]).astype(BF)
    store(1, f1)
    r2 = r2 - mm(f0, l20) - mm(f1, l21)
    f2 = mm(r2.astype(BF), dt_odd[0]).astype(BF)
    store(2, f2)
    r3 = r3 - mm(f0, l30) - mm(f1, l31) - mm(f2, l32)
    f3 = mm(r3.astype(BF), dt_odd[1]).astype(BF)
    store(3, f3)


def finish_kernel(info, r, a, l_own, l_oth, dg_own, dg_oth, dt_own, dt_oth, every_in, f, every, acc, sem):
    step = pl.program_id(0)
    plane, core, slot, valid = info[0], info[1], info[3], info[4]
    size = a.shape[2]

    @pl.when(step == 0)
    def _():
        acc[...] = r[0]

    @pl.when((plane > 0) & (valid == 1))
    def _():
        for where, block in ((core, l_own), (1 - core, l_oth)):
            acc[pl.ds(where, 1)] -= mm(a[0], block[...].reshape(size, -1))[None]

    @pl.when((step == pl.num_programs(0) - 1) & (valid == 1))
    def _():
        def store(i, value):
            f[i // 2, :, (i % 2) * size:(i % 2 + 1) * size] = value

        @pl.when(core == 0)
        def _():
            solve(acc, dg_own, dg_oth, dt_own, dt_oth, store)

        @pl.when(core == 1)
        def _():
            solve(acc, dg_oth, dg_own, dt_oth, dt_own, store)

    @pl.when(step == pl.num_programs(0) - 1)
    def _():
        out = pltpu.make_async_copy(f, every.at[slot], sem)
        out.start()
        out.wait()


def early_kernel(info, r, own, b, c, l_own, l_oth, r_out, p, acc):
    step = pl.program_id(0)
    plane, core, valid = info[0], info[1], info[3]
    size = b.shape[2]

    @pl.when(step == 0)
    def _():
        acc[...] = jnp.zeros_like(acc)

    def add(source):
        for where, block in ((core, l_own), (1 - core, l_oth)):
            acc[pl.ds(where, 1)] += mm(source[0], block[...].reshape(size, -1))[None]

    @pl.when((valid == 1) & (plane == 0))
    def _():
        add(own)

    @pl.when((valid == 1) & (plane >= 2))
    def _():
        add(b)

    @pl.when(step == pl.num_programs(0) - 1)
    def _():
        p[...] = acc[...].astype(BF)

        @pl.when((valid == 1) & (plane == 2))
        def _():
            r_out[0] = r[0] - acc[...]

        @pl.when((valid == 1) & (plane == 3))
        def _():
            r_out[0] = r[0] - acc[...] - c[...].astype(F32)

        @pl.when((valid == 0) | (plane < 2))
        def _():
            r_out[0] = r[0]


def params():
    return pltpu.CompilerParams(dimension_semantics=("arbitrary",), vmem_limit_bytes=48 << 20)


def per_device(embeddings, landmarks, factor_rows, diag_inverse):
    tokens, depth = embeddings.shape
    rows = lax.axis_size("rows")
    planes = lax.axis_size("cols") // 2
    here = lax.axis_index("cols")
    plane, core = here // 2, here % 2
    own_rows, blocks, slab = factor_rows.shape
    size = diag_inverse.shape[1]
    n = CHUNKS
    t = tokens // 2 // n
    scale = 0.5 / math.sqrt(depth)
    per_plane = blocks // planes

    def shift(x, by, sources):
        pairs = [(2 * z + k, 2 * ((z + by) % planes) + k) for z in sources for k in range(2)]
        return lax.ppermute(x, "cols", pairs)

    def swap(x):
        return lax.ppermute(x, "cols", [(c, c ^ 1) for c in range(2 * planes)])

    ft = factor_rows.transpose(1, 2, 0)
    first = shift(ft[:per_plane], -3, [3])
    dt_own = diag_inverse.transpose(0, 2, 1)
    dt_oth = swap(dt_own)
    mine = lax.dynamic_slice_in_dim(ft, per_plane * plane, per_plane, 0)
    to_even = lax.ppermute(mine[2, :, size:], "cols", [(2 * z + 1, 2 * z) for z in range(planes)])
    even_diag = jnp.stack([jnp.concatenate([mine[0, :, size:], to_even], axis=1), mine[1]])
    diag = jnp.where(core == 0, even_diag, mine[:2])
    head = jnp.concatenate([landmarks.T, diag.reshape(2 * slab, own_rows)], axis=0)

    def gather(x):
        return lax.all_gather(x, "rows", axis=0, tiled=False)

    head_own = gather(head)
    late = gather(lax.dynamic_slice_in_dim(ft, per_plane * jnp.maximum(plane - 1, 0), per_plane, 0))
    early_shard = jnp.where(
        plane == 0, first, lax.dynamic_slice_in_dim(ft, per_plane * jnp.maximum(plane - 2, 0), per_plane, 0)
    )
    early = gather(early_shard)
    head_oth = swap(head_own)
    late_oth = swap(late)
    early_oth = swap(early)

    lead = landmarks.shape[1]
    emb = lax.dynamic_slice_in_dim(embeddings, core * (tokens // 2), tokens // 2, 0)
    where = jnp.stack([plane, core]).astype(jnp.int32)
    whole = lambda *shape: pl.BlockSpec(shape, lambda i, s: (0,) * len(shape))
    running = pl.pallas_call(
        functools.partial(scores_kernel, scale),
        grid_spec=pltpu.PrefetchScalarGridSpec(
            num_scalar_prefetch=1,
            grid=(n,),
            in_specs=[
                pl.BlockSpec((t, depth), lambda i, s: (i, 0)),
                whole(rows, lead, own_rows),
                whole(rows, lead, own_rows),
            ],
            out_specs=pl.BlockSpec((1, 2, t, own_rows), lambda i, s: (i, 0, 0, 0)),
        ),
        out_shape=jax.ShapeDtypeStruct((n, 2, t, own_rows), F32),
        compiler_params=params(),
        name="scores",
    )(where, emb, head_own, head_oth)

    f_spec = pl.BlockSpec((1, t, size), lambda k, s: (k // 2, 0, k % 2))
    l_spec = pl.BlockSpec((rows, 1, slab, own_rows), lambda k, s: (0, k, 0, 0))
    r_spec = pl.BlockSpec((1, 2, t, own_rows), lambda k, s: (s[2], 0, 0, 0))
    dg_spec = pl.BlockSpec((rows, 2 * slab, own_rows), lambda k, s: (0, lead // (2 * slab), 0))
    flops = 2 * t * per_plane * size * 2 * own_rows

    def finish(step, running, arrived, every):
        chunk = step - plane
        valid = (chunk >= 0) & (chunk < n)
        info = jnp.stack([plane, core, jnp.clip(chunk, 0, n - 1), jnp.where(valid, chunk, n), valid]).astype(jnp.int32)
        return pl.pallas_call(
            finish_kernel,
            grid_spec=pltpu.PrefetchScalarGridSpec(
                num_scalar_prefetch=1,
                grid=(per_plane,),
                in_specs=[
                    r_spec, f_spec, l_spec, l_spec, dg_spec, dg_spec,
                    whole(2, size, size), whole(2, size, size),
                    pl.BlockSpec(memory_space=pl.ANY),
                ],
                out_specs=[whole(2, t, own_rows), pl.BlockSpec(memory_space=pl.ANY)],
                scratch_shapes=[pltpu.VMEM((2, t, own_rows), F32), pltpu.SemaphoreType.DMA],
            ),
            out_shape=[
                jax.ShapeDtypeStruct((2, t, own_rows), BF),
                jax.ShapeDtypeStruct((n + 1, 2, t, own_rows), BF),
            ],
            input_output_aliases={9: 1},
            compiler_params=params(),
            cost_estimate=pl.CostEstimate(flops=flops * 2, bytes_accessed=24 << 20, transcendentals=0),
            name="finish",
        )(info, running, arrived, late, late_oth, head_own, head_oth, dt_own, dt_oth, every)

    def ahead(step, running, own, arrived, partial):
        chunk = jnp.where(plane == 0, step, step + 1 - plane)
        valid = (chunk >= 0) & (chunk < n) & (plane != 1)
        info = jnp.stack([plane, core, jnp.clip(chunk, 0, n - 1), valid]).astype(jnp.int32)
        return pl.pallas_call(
            early_kernel,
            grid_spec=pltpu.PrefetchScalarGridSpec(
                num_scalar_prefetch=1,
                grid=(per_plane,),
                in_specs=[r_spec, f_spec, f_spec, whole(2, t, own_rows), l_spec, l_spec],
                out_specs=[r_spec, whole(2, t, own_rows)],
                scratch_shapes=[pltpu.VMEM((2, t, own_rows), F32)],
            ),
            out_shape=[
                jax.ShapeDtypeStruct((n, 2, t, own_rows), F32),
                jax.ShapeDtypeStruct((2, t, own_rows), BF),
            ],
            input_output_aliases={1: 0},
            compiler_params=params(),
            cost_estimate=pl.CostEstimate(flops=flops, bytes_accessed=20 << 20, transcendentals=0),
            name="ahead",
        )(info, running, own, arrived, partial, early, early_oth)

    none = jnp.zeros((2, t, own_rows), BF)
    every = jnp.zeros((n + 1, 2, t, own_rows), BF)
    one_back = none
    two_back = none
    partials = []
    for step in range(n + planes - 1):
        f, every = finish(step, running, one_back, every)
        active = [z for z in range(planes) if 0 <= step - z < n]
        if step == n + planes - 2:
            break
        near = [z for z in active if z + 1 < planes]
        far = [z for z in active if z + 2 < planes]
        partial = partials[step - 2] if 0 <= step - 2 < len(partials) else none
        one_back = shift(f, 1, near)
        next_two = shift(f, 2, far) if far else none
        running, p = ahead(step, running, f, two_back, partial)
        if step < n:
            partials.append(shift(p, -1, [0]))
        two_back = next_two

    done = every[:n]
    keep = lax.dynamic_index_in_dim(done, core, 1, False).reshape(n * t, own_rows)
    give = lax.dynamic_index_in_dim(done, 1 - core, 1, False).reshape(n * t, own_rows)
    got = swap(give)
    return jnp.where(
        core == 0, jnp.concatenate([keep, got], axis=0), jnp.concatenate([got, keep], axis=0)
    )


def solution(mesh):
    in_specs = (P("rows", None), P("cols", "rows"), P("cols", None, "rows"), P("cols", None, None))
    out_specs = P("rows", "cols")
    return jax.shard_map(
        per_device, mesh=mesh, in_specs=in_specs, out_specs=out_specs, check_vma=False
    )
```

```python
import functools
import math

import jax
import jax.numpy as jnp
from jax import lax
from jax.experimental import pallas as pl
from jax.experimental.pallas import tpu as pltpu
from jax.sharding import PartitionSpec as P

CHUNKS = 2
SIDE = 4
BF = jnp.bfloat16
F32 = jnp.float32
ANY = pl.BlockSpec(memory_space=pl.ANY)
SMEM = pl.BlockSpec(memory_space=pltpu.SMEM)
VMEM = pl.BlockSpec(memory_space=pltpu.VMEM)


def mm(a, b):
    return jnp.dot(a, b, preferred_element_type=F32)


def after(x, *deps):
    return lax.optimization_barrier((x, *deps))[0]


PIECES = ((0, (0, 1, 2, 3)), (1, (0, 1, 2, 3)), (3, (0, 1, 2, 3)), (2, (0, 1)), (2, (2, 3)))
N_PIECES = 2 * len(PIECES)


def piece_places(info):
    core, y, x = info[1], info[2], info[3]
    for which, parity in ((0, core), (1, 1 - core)):
        for i, (e, along) in enumerate(PIECES):
            for j, d in enumerate(along):
                dy, dx = jnp.where(parity == 0, e, d), jnp.where(parity == 0, d, e)
                yield which * len(PIECES) + i, j, parity, ((y + dy) % SIDE) * SIDE + (x + dx) % SIDE


def start_diag(info, head, dt_own, dt_oth, gv, dv, sem):
    core = info[1]
    depth = gv.shape[2]
    pltpu.make_async_copy(head.at[:, :, pl.ds(head.shape[2] - depth, depth)], gv, sem.at[0]).start()
    pltpu.make_async_copy(dt_own, dv.at[core], sem.at[1]).start()
    pltpu.make_async_copy(dt_oth, dv.at[1 - core], sem.at[1]).start()


def wait_diag(gv, dv, sem):
    pltpu.make_async_copy(gv, gv, sem.at[0]).wait()
    pltpu.make_async_copy(dv, dv, sem.at[1]).wait()


def solve(running, diag, dt, f):
    size = dt.shape[-1]

    def column(i):
        return running[i // 2, :, (i % 2) * size:(i % 2 + 1) * size]

    def store(i, value):
        f[i // 2, :, (i % 2) * size:(i % 2 + 1) * size] = value

    def left(i, k):
        slab = diag.shape[2] // 3
        block = diag[i // 2, :, k * slab:(k + 1) * slab, (i % 2) * size:(i % 2 + 1) * size]
        return block.reshape(size, size)

    f0 = mm(column(0).astype(BF), dt[0, 0]).astype(BF)
    store(0, f0)
    f1 = mm((column(1) - mm(f0, left(1, 0))).astype(BF), dt[0, 1]).astype(BF)
    store(1, f1)
    f2 = mm((column(2) - mm(f0, left(2, 0)) - mm(f1, left(2, 1))).astype(BF), dt[1, 0]).astype(BF)
    store(2, f2)
    f3 = column(3) - mm(f0, left(3, 0)) - mm(f1, left(3, 1)) - mm(f2, left(3, 2))
    store(3, mm(f3.astype(BF), dt[1, 1]).astype(BF))


def pick_kernel(info, first, other, out):
    out[...] = jnp.where(info[0] == 1, first[...], other[...])


def scores_kernel(scale, info, emb, dt_own, dt_oth, head, *refs):
    out, f, (lm, gv, dv, sem) = refs[:CHUNKS], refs[CHUNKS:2 * CHUNKS], refs[2 * CHUNKS:]
    plane = info[0]
    lead = lm.shape[2]
    t = out[0].shape[1]
    copies = [pltpu.make_async_copy(head.at[i, :, pl.ds(0, lead)], lm.at[i], sem.at[2 + i]) for i in range(2)]
    for copy in copies:
        copy.start()
    pl.when(plane == 0)(lambda: start_diag(info, head, dt_own, dt_oth, gv, dv, sem))
    for half in range(2):
        copies[half].wait()
        points = lm[half].reshape(emb.shape[1], lm.shape[3])
        for q in range(CHUNKS):
            out[q][half] = jnp.exp(mm(emb[q * t:(q + 1) * t, :], points) * scale)

    @pl.when(plane == 0)
    def _():
        wait_diag(gv, dv, sem)
        for q in range(CHUNKS):
            solve(out[q], gv, dv, f[q])


def start_factor(factor, lv, sems):
    copies = []
    for half in range(2):
        copies.append(pltpu.make_async_copy(factor.at[half], lv.at[half], sems.at[half]))
        copies[-1].start()
    return copies


def subtract(acc, av, lv, copies):
    size = lv.shape[1] * lv.shape[3]
    for half in range(2):
        copies[half].wait()
        for k in range(lv.shape[2]):
            left = av[k // 2, :, (k % 2) * size:(k % 2 + 1) * size]
            acc[half] -= mm(left, lv[half, :, k].reshape(size, -1))


def finish_kernel(role, q, info, r, a, head, dt_own, dt_oth, *refs):
    last = role == SIDE - 1
    pieces, refs = refs[:N_PIECES], refs[N_PIECES:]
    if last:
        part, earlier, refs = refs[0], refs[1:SIDE], refs[SIDE:]
        keep, give, f, pv, acc, av, lv, gv, dv, sems, sem = refs
    else:
        f, acc, av, lv, gv, dv, sems, sem = refs
    plane, core = info[0], info[1]
    t = acc.shape[1]

    @pl.when(plane == role)
    def _():
        ca = pltpu.make_async_copy(a, av, sems.at[2])
        cr = pltpu.make_async_copy(r, acc, sems.at[3])
        ca.start()
        cr.start()
        for i, d, parity, place in piece_places(info):
            pltpu.make_async_copy(pieces[i].at[d], lv.at[parity, place], sems.at[parity]).start()
        start_diag(info, head, dt_own, dt_oth, gv, dv, sem)
        if last:
            cp = pltpu.make_async_copy(part.at[:, pl.ds(q * t, t)], pv, sems.at[6])
            cp.start()
        ca.wait()
        cr.wait()
        if last:
            cp.wait()
            acc[...] += pv[...].astype(F32)
        subtract(acc, av, lv, [pltpu.make_async_copy(lv.at[half], lv.at[half], sems.at[half]) for half in range(2)])
        wait_diag(gv, dv, sem)
        solve(acc, gv, dv, f)
        if last:
            keep[...] = f[pl.ds(core, 1)][0]
            give[...] = f[pl.ds(1 - core, 1)][0]

    if last:
        for z, done in enumerate(earlier):

            @pl.when(plane == z)
            def _():
                c0 = pltpu.make_async_copy(done.at[core], keep, sems.at[0])
                c1 = pltpu.make_async_copy(done.at[1 - core], give, sems.at[1])
                c0.start()
                c1.start()
                c0.wait()
                c1.wait()


def partial_kernel(info, factor, *refs):
    own, (p, acc, av, lv, sems) = refs[:CHUNKS], refs[CHUNKS:]
    t = own[0].shape[1]

    @pl.when(info[0] == 1)
    def _():
        moves = [pltpu.make_async_copy(own[q], av.at[:, pl.ds(q * t, t)], sems.at[2 + q]) for q in range(CHUNKS)]
        for move in moves:
            move.start()
        copies = start_factor(factor, lv, sems)
        acc[...] = jnp.zeros_like(acc)
        for move in moves:
            move.wait()
        subtract(acc, av, lv, copies)
        p[...] = acc[...].astype(BF)


def update_kernel(info, factor, r, to_3, to_2, r_out, acc, av, lv, sems):
    @pl.when(info[0] >= 2)
    def _():
        copies = start_factor(factor, lv, sems)
        cr = pltpu.make_async_copy(r, acc, sems.at[2])
        cr.start()
        for plane, a in ((2, to_2), (3, to_3)):
            pl.when(info[0] == plane)(lambda a=a: pltpu.make_async_copy(a, av, sems.at[3]).start())
        cr.wait()
        pltpu.make_async_copy(to_2, av, sems.at[3]).wait()
        subtract(acc, av, lv, copies)
        out = pltpu.make_async_copy(acc, r_out, sems.at[2])
        out.start()
        out.wait()


def params(mib=60):
    return pltpu.CompilerParams(vmem_limit_bytes=mib << 20)


def cost(us):
    return pl.CostEstimate(flops=us * 1_000_000_000, bytes_accessed=1 << 10, transcendentals=0)


def per_device(embeddings, landmarks, factor_rows, diag_inverse):
    tokens, depth = embeddings.shape
    rows = lax.axis_size("rows")
    planes = lax.axis_size("cols") // 2
    here = lax.axis_index("cols")
    plane, core = here // 2, here % 2
    row = lax.axis_index("rows")
    own_rows, blocks, slab = factor_rows.shape
    size = diag_inverse.shape[1]
    lead = landmarks.shape[1]
    n = CHUNKS
    half = tokens // 2
    t = half // n
    scale = 0.5 / math.sqrt(depth)
    per_plane = blocks // planes
    info = jnp.stack([plane, core, row // SIDE, row % SIDE]).astype(jnp.int32)

    def send(x, source, target):
        return lax.ppermute(x, "cols", [(2 * source + k, 2 * target + k) for k in range(2)])

    def swap(x):
        return lax.ppermute(x, "cols", [(c, c ^ 1) for c in range(2 * planes)])

    def fetch(x, by, second):
        pairs = []
        for y in range(SIDE):
            for q in range(SIDE):
                for c in range(2, 2 * planes):
                    along_x = (c % 2 == 0) != second
                    sy, sx = (y, (q + by) % SIDE) if along_x else ((y + by) % SIDE, q)
                    pairs.append(((sy * SIDE + sx) * 2 * planes + c, (y * SIDE + q) * 2 * planes + c))
        return lax.ppermute(x, ("rows", "cols"), pairs)

    def line_of(x):
        return jnp.stack([x] + [fetch(x, by, False) for by in range(1, SIDE)])

    def spread(line):
        up, down = fetch(line, 1, True), fetch(line, 3, True)
        mid = SIDE // 2
        return [line, up, down, fetch(up[:mid], 1, True), fetch(down[mid:], 3, True)]

    ft = factor_rows.transpose(1, 2, 0)
    groups = [[r * 2 * planes + 2 * z + k for k in range(2) for r in range(rows)] for z in range(planes)]

    def gather(x):
        everyone = lax.all_gather(x, ("rows", "cols"), axis=0, axis_index_groups=groups)
        return everyone.reshape(2, rows, *x.shape)

    diag = lax.dynamic_slice_in_dim(ft, per_plane * plane, per_plane - 1, 0)
    head = gather(jnp.concatenate([landmarks.T, diag.reshape(-1, own_rows)], axis=0))
    dt_own = diag_inverse.transpose(0, 2, 1)
    dt_oth = swap(dt_own)

    late = line_of(lax.dynamic_slice_in_dim(ft, per_plane * jnp.maximum(plane - 1, 0), per_plane, 0))
    late = spread(late)

    first = send(after(ft[per_plane:2 * per_plane], *late[1:3]), 3, 1)
    factor = gather(
        pl.pallas_call(
            pick_kernel,
            in_specs=[SMEM, VMEM, VMEM],
            out_specs=VMEM,
            out_shape=jax.ShapeDtypeStruct(first.shape, BF),
            cost_estimate=cost(60),
            name="pick",
        )(info, first, ft[:per_plane])
    )

    emb = lax.dynamic_slice_in_dim(embeddings, core * half, half, 0)
    chunk_f32 = jax.ShapeDtypeStruct((2, t, own_rows), F32)
    chunk_bf = jax.ShapeDtypeStruct((2, t, own_rows), BF)
    whole_bf = jax.ShapeDtypeStruct((2, half, own_rows), BF)
    diag_scratch = [
        pltpu.VMEM((2, rows, (per_plane - 1) * slab, own_rows), BF),
        pltpu.VMEM((2, 2, size, size), BF),
    ]
    factor_scratch = [
        pltpu.VMEM(whole_bf.shape, F32),
        pltpu.VMEM(whole_bf.shape, BF),
        pltpu.VMEM((2, rows, per_plane, slab, own_rows), BF),
        pltpu.SemaphoreType.DMA((7,)),
    ]
    out = pl.pallas_call(
        functools.partial(scores_kernel, scale),
        in_specs=[SMEM, VMEM] + [ANY] * 3,
        out_specs=[VMEM] * (2 * n),
        out_shape=[chunk_f32] * n + [chunk_bf] * n,
        scratch_shapes=[pltpu.VMEM((2, rows, lead, own_rows), BF)] + diag_scratch + [pltpu.SemaphoreType.DMA((4,))],
        compiler_params=params(),
        cost_estimate=cost(3),
        name="scores",
    )(info, after(emb, *late[:3]), dt_own, dt_oth, head)
    r, f0 = out[:n], out[n:]
    f0_to_1 = [send(x, 0, 1) for x in f0]
    f0_to_3 = [send(x, 0, 3) for x in f0]
    f0_to_2 = [send(x, 3, 2) for x in f0_to_3]
    late = late + [swap(x) for x in late]
    factor = after(factor, f0[-1])

    def finish(role, q, r, a, more=()):
        last = role == planes - 1
        one = jax.ShapeDtypeStruct((t, own_rows), BF)
        return pl.pallas_call(
            functools.partial(finish_kernel, role, q),
            in_specs=[SMEM] + [ANY] * (5 + N_PIECES + len(more)),
            out_specs=[VMEM] * 2 if last else VMEM,
            out_shape=[one, one] if last else chunk_bf,
            scratch_shapes=([pltpu.VMEM(chunk_bf.shape, BF)] * 2 if last else [])
            + [pltpu.VMEM(chunk_f32.shape, F32), pltpu.VMEM(chunk_bf.shape, BF), factor_scratch[2]]
            + diag_scratch
            + [factor_scratch[3], pltpu.SemaphoreType.DMA((2,))],
            compiler_params=params(),
            cost_estimate=cost(3),
            name=f"finish{role}",
        )(info, r, a, head, dt_own, dt_oth, *late, *more)

    def partial(own):
        return pl.pallas_call(
            partial_kernel,
            in_specs=[SMEM] + [ANY] * (1 + n),
            out_specs=VMEM,
            out_shape=whole_bf,
            scratch_shapes=factor_scratch,
            compiler_params=params(),
            cost_estimate=cost(0),
            name="partial",
        )(info, factor, *own)

    def update(r, to_3, to_2):
        return pl.pallas_call(
            update_kernel,
            in_specs=[SMEM] + [ANY] * 4,
            out_specs=ANY,
            out_shape=chunk_f32,
            scratch_shapes=[
                pltpu.VMEM(chunk_f32.shape, F32),
                pltpu.VMEM(chunk_bf.shape, BF),
            ]
            + factor_scratch[2:],
            compiler_params=params(),
            cost_estimate=cost(0),
            name="update",
        )(info, factor, r, to_3, to_2)

    f1 = []
    for q in range(n):
        f1.append(finish(1, q, r[q], after(f0_to_1[q], *f1)))
    f1_to_2 = [send(x, 1, 2) for x in f1]
    part = send(partial(f1), 1, 3)
    r2, f2 = [], []
    for q in range(n):
        r2.append(update(r[q], f0_to_3[q], after(f0_to_2[q], f1[-1], *f2)))
        f2.append(finish(2, q, r2[q], f1_to_2[q]))
    f2_to_3 = [send(x, 2, 3) for x in f2]
    done = []
    for q in range(n):
        a = after(f2_to_3[q], *[x[0] for x in done])
        done.append(finish(3, q, r2[q], a, (part, f0[q], f1[q], f2[q])))
    keep = [x for x, _ in done]
    got = [swap(x) for _, x in done]
    return jnp.where(core == 0, jnp.concatenate(keep + got, axis=0), jnp.concatenate(got + keep, axis=0))


def solution(mesh):
    in_specs = (P("rows", None), P("cols", "rows"), P("cols", None, "rows"), P("cols", None, None))
    out_specs = P("rows", "cols")
    return jax.shard_map(
        per_device, mesh=mesh, in_specs=in_specs, out_specs=out_specs, check_vma=False
    )
```

```python
import functools
import math

import jax
import jax.numpy as jnp
from jax import lax
from jax.experimental import pallas as pl
from jax.experimental.pallas import tpu as pltpu
from jax.sharding import PartitionSpec as P

CHUNKS = 2
SIDE = 4
LEAD = 64
SLAB = 32
BF = jnp.bfloat16
F32 = jnp.float32
ANY = pl.BlockSpec(memory_space=pl.ANY)
SMEM = pl.BlockSpec(memory_space=pltpu.SMEM)
VMEM = pl.BlockSpec(memory_space=pltpu.VMEM)


def mm(a, b):
    return jnp.dot(a, b, preferred_element_type=F32)


def after(x, *deps):
    return lax.optimization_barrier((x, *deps))[0]


def start_diag(info, head, dt_own, dt_oth, gv, dv, sem):
    core = info[1]
    depth = gv.shape[2]
    pltpu.make_async_copy(head.at[:, :, pl.ds(LEAD, depth)], gv, sem.at[0]).start()
    pltpu.make_async_copy(dt_own, dv.at[core], sem.at[1]).start()
    pltpu.make_async_copy(dt_oth, dv.at[1 - core], sem.at[1]).start()


def wait_diag(gv, dv, sem):
    pltpu.make_async_copy(gv, gv, sem.at[0]).wait()
    pltpu.make_async_copy(dv, dv, sem.at[1]).wait()


def solve(running, diag, dt, f):
    size = dt.shape[-1]

    def column(i):
        return running[i // 2, :, (i % 2) * size:(i % 2 + 1) * size]

    def store(i, value):
        f[i // 2, :, (i % 2) * size:(i % 2 + 1) * size] = value

    def left(i, k):
        block = diag[i // 2, :, k * SLAB:(k + 1) * SLAB, (i % 2) * size:(i % 2 + 1) * size]
        return block.reshape(size, size)

    f0 = mm(column(0).astype(BF), dt[0, 0]).astype(BF)
    store(0, f0)
    f1 = mm((column(1) - mm(f0, left(1, 0))).astype(BF), dt[0, 1]).astype(BF)
    store(1, f1)
    f2 = mm((column(2) - mm(f0, left(2, 0)) - mm(f1, left(2, 1))).astype(BF), dt[1, 0]).astype(BF)
    store(2, f2)
    f3 = column(3) - mm(f0, left(3, 0)) - mm(f1, left(3, 1)) - mm(f2, left(3, 2))
    store(3, mm(f3.astype(BF), dt[1, 1]).astype(BF))


def hold_kernel(x, token, out):
    pass


def pick_kernel(info, first, other, out):
    out[...] = jnp.where(info[0] == 1, first[...], other[...])


def scores_kernel(scale, info, emb, dt_own, dt_oth, head, out, f, lm, gv, dv, sem):
    plane = info[0]
    lead = lm.shape[2]
    copies = [pltpu.make_async_copy(head.at[i, :, pl.ds(0, lead)], lm.at[i], sem.at[2 + i]) for i in range(2)]
    for copy in copies:
        copy.start()
    pl.when(plane == 0)(lambda: start_diag(info, head, dt_own, dt_oth, gv, dv, sem))
    for half in range(2):
        copies[half].wait()
        points = lm[half].reshape(emb.shape[1], lm.shape[3])
        out[half] = jnp.exp(mm(emb[...], points) * scale)

    @pl.when(plane == 0)
    def _():
        wait_diag(gv, dv, sem)
        solve(out, gv, dv, f)


def start_factor(factor, lv, sems):
    depth = lv.shape[2]
    copies = []
    for half in range(2):
        part = factor.at[half, :, pl.ds(factor.shape[2] - depth, depth)]
        copies.append(pltpu.make_async_copy(part, lv.at[half], sems.at[half]))
        copies[-1].start()
    return copies


def subtract(acc, av, lv, copies):
    size = lv.shape[1] * SLAB
    for half in range(2):
        copies[half].wait()
        for k in range(lv.shape[2] // SLAB):
            left = av[k // 2, :, (k % 2) * size:(k % 2 + 1) * size]
            acc[half] -= mm(left, lv[half, :, k * SLAB:(k + 1) * SLAB].reshape(size, -1))


def finish_kernel(role, info, r, a, head, dt_own, dt_oth, factor, *refs):
    last = role == SIDE - 1
    if last:
        part, earlier, refs = refs[0], refs[1:SIDE], refs[SIDE:]
        keep, give, f, pv, acc, av, lv, gv, dv, sems, sem = refs
    else:
        f, acc, av, lv, gv, dv, sems, sem = refs
    plane, core = info[0], info[1]

    @pl.when(plane == role)
    def _():
        ca = pltpu.make_async_copy(a, av, sems.at[2])
        cr = pltpu.make_async_copy(r, acc, sems.at[3])
        ca.start()
        cr.start()
        copies = start_factor(factor, lv, sems)
        start_diag(info, head, dt_own, dt_oth, gv, dv, sem)
        if last:
            cp = pltpu.make_async_copy(part, pv, sems.at[6])
            cp.start()
        ca.wait()
        cr.wait()
        if last:
            cp.wait()
            acc[...] += pv[...].astype(F32)
        subtract(acc, av, lv, copies)
        wait_diag(gv, dv, sem)
        solve(acc, gv, dv, f)
        if last:
            keep[...] = f[pl.ds(core, 1)][0]
            give[...] = f[pl.ds(1 - core, 1)][0]

    if last:
        for z, done in enumerate(earlier):

            @pl.when(plane == z)
            def _():
                c0 = pltpu.make_async_copy(done.at[core], keep, sems.at[0])
                c1 = pltpu.make_async_copy(done.at[1 - core], give, sems.at[1])
                c0.start()
                c1.start()
                c0.wait()
                c1.wait()


def partial_kernel(info, factor, own, p, acc, av, lv, sems):
    @pl.when(info[0] == 1)
    def _():
        ca = pltpu.make_async_copy(own, av, sems.at[2])
        ca.start()
        copies = start_factor(factor, lv, sems)
        acc[...] = jnp.zeros_like(acc)
        ca.wait()
        subtract(acc, av, lv, copies)
        p[...] = acc[...].astype(BF)


def update_kernel(info, head, r, to_3, to_2, r_out, acc, av, lv, sems):
    @pl.when(info[0] >= 2)
    def _():
        copies = start_factor(head, lv, sems)
        cr = pltpu.make_async_copy(r, acc, sems.at[2])
        cr.start()
        for plane, a in ((2, to_2), (3, to_3)):
            pl.when(info[0] == plane)(lambda a=a: pltpu.make_async_copy(a, av, sems.at[3]).start())
        cr.wait()
        pltpu.make_async_copy(to_2, av, sems.at[3]).wait()
        subtract(acc, av, lv, copies)
        out = pltpu.make_async_copy(acc, r_out, sems.at[2])
        out.start()
        out.wait()


def params(mib=60):
    return pltpu.CompilerParams(vmem_limit_bytes=mib << 20)


def cost(us):
    return pl.CostEstimate(flops=int(us * 1e9), bytes_accessed=1 << 10, transcendentals=0)


def per_device(embeddings, landmarks, factor_rows, diag_inverse):
    tokens, depth = embeddings.shape
    rows = lax.axis_size("rows")
    planes = lax.axis_size("cols") // 2
    here = lax.axis_index("cols")
    plane, core = here // 2, here % 2
    row = lax.axis_index("rows")
    own_rows, blocks, slab = factor_rows.shape
    size = diag_inverse.shape[1]
    lead = landmarks.shape[1]
    n = CHUNKS
    half = tokens // 2
    t = half // n
    scale = 0.5 / math.sqrt(depth)
    per_plane = blocks // planes
    info = jnp.stack([plane, core, row // SIDE, row % SIDE]).astype(jnp.int32)

    def send(x, source, target):
        return lax.ppermute(x, "cols", [(2 * source + k, 2 * target + k) for k in range(2)])

    def swap(x):
        return lax.ppermute(x, "cols", [(c, c ^ 1) for c in range(2 * planes)])

    ft = factor_rows.transpose(1, 2, 0)
    groups = [[r * 2 * planes + 2 * z + k for k in range(2) for r in range(rows)] for z in range(planes)]

    def gather(x):
        everyone = lax.all_gather(x, ("rows", "cols"), axis=0, axis_index_groups=groups)
        return everyone.reshape(2, rows, *x.shape)

    diag = lax.dynamic_slice_in_dim(ft, per_plane * plane, per_plane - 1, 0)
    head = gather(
        jnp.concatenate([landmarks.T, diag.reshape(-1, own_rows), ft[:per_plane].reshape(-1, own_rows)], axis=0)
    )
    dt_own = diag_inverse.transpose(0, 2, 1)
    dt_oth = swap(dt_own)

    first = send(ft[per_plane:2 * per_plane], 3, 1)
    other = lax.dynamic_slice_in_dim(ft, per_plane * jnp.maximum(plane - 1, 0), per_plane, 0)
    factor = gather(
        pl.pallas_call(
            pick_kernel,
            in_specs=[SMEM, VMEM, VMEM],
            out_specs=VMEM,
            out_shape=jax.ShapeDtypeStruct((per_plane * slab, own_rows), BF),
            cost_estimate=cost(0),
            name="pick",
        )(info, first.reshape(-1, own_rows), other.reshape(-1, own_rows))
    )

    emb = lax.dynamic_slice_in_dim(embeddings, core * half, half, 0)
    chunk_f32 = jax.ShapeDtypeStruct((2, t, own_rows), F32)
    chunk_bf = jax.ShapeDtypeStruct((2, t, own_rows), BF)
    whole_bf = jax.ShapeDtypeStruct((2, half, own_rows), BF)
    diag_scratch = [
        pltpu.VMEM((2, rows, (per_plane - 1) * slab, own_rows), BF),
        pltpu.VMEM((2, 2, size, size), BF),
    ]
    factor_scratch = [
        pltpu.VMEM(chunk_f32.shape, F32),
        pltpu.VMEM(chunk_bf.shape, BF),
        pltpu.VMEM((2, rows, per_plane * slab, own_rows), BF),
        pltpu.SemaphoreType.DMA((7,)),
    ]
    r, f0 = [], []
    for q in range(n):
        x = emb[q * t:(q + 1) * t]
        out = pl.pallas_call(
            functools.partial(scores_kernel, scale),
            in_specs=[SMEM, VMEM] + [ANY] * 3,
            out_specs=[VMEM] * 2,
            out_shape=[chunk_f32, chunk_bf],
            scratch_shapes=[pltpu.VMEM((2, rows, lead, own_rows), BF)]
            + diag_scratch
            + [pltpu.SemaphoreType.DMA((4,))],
            compiler_params=params(),
            cost_estimate=cost(100),
            name="scores",
        )(info, after(x, f0[-1]) if q else x, dt_own, dt_oth, head)
        r.append(out[0])
        f0.append(out[1])
    f0_to_1 = [send(x, 0, 1) for x in f0]
    f0_to_3 = [send(x, 0, 3) for x in f0]
    f0_to_2 = [send(x, 3, 2) for x in f0_to_3]
    r[0] = pl.pallas_call(
        hold_kernel,
        in_specs=[ANY, ANY],
        out_specs=ANY,
        out_shape=chunk_f32,
        input_output_aliases={0: 0},
        cost_estimate=cost(100),
        name="hold",
    )(r[0], f0[-1])

    def finish(role, r, a, more=()):
        last = role == planes - 1
        one = jax.ShapeDtypeStruct((t, own_rows), BF)
        return pl.pallas_call(
            functools.partial(finish_kernel, role),
            in_specs=[SMEM] + [ANY] * (6 + len(more)),
            out_specs=[VMEM] * 2 if last else VMEM,
            out_shape=[one, one] if last else chunk_bf,
            scratch_shapes=([pltpu.VMEM(chunk_bf.shape, BF)] * 2 if last else [])
            + factor_scratch[:3]
            + diag_scratch
            + [factor_scratch[3], pltpu.SemaphoreType.DMA((2,))],
            compiler_params=params(),
            cost_estimate=cost(0.8),
            name=f"finish{role}",
        )(info, r, a, head, dt_own, dt_oth, head if role == 1 else factor, *more)

    def partial(own):
        return pl.pallas_call(
            partial_kernel,
            in_specs=[SMEM] + [ANY] * 2,
            out_specs=VMEM,
            out_shape=chunk_bf,
            scratch_shapes=factor_scratch,
            compiler_params=params(),
            cost_estimate=cost(0),
            name="partial",
        )(info, factor, own)

    def update(r, to_3, to_2):
        return pl.pallas_call(
            update_kernel,
            in_specs=[SMEM] + [ANY] * 4,
            out_specs=ANY,
            out_shape=chunk_f32,
            scratch_shapes=factor_scratch,
            compiler_params=params(),
            cost_estimate=cost(0),
            name="update",
        )(info, head, r, to_3, to_2)

    f1, parts = [], []
    for q in range(n):
        f1.append(finish(1, r[q], after(f0_to_1[q], *f1)))
    f1_to_2 = [send(x, 1, 2) for x in f1]
    r2, f2 = [], []
    for q in range(n):
        r2.append(update(r[q], f0_to_3[q], after(f0_to_2[q], f1[-1], *f2)))
        if q == 0:
            for i in range(n):
                parts.append(partial(after(f1[i], r2[0], *parts)))
        f2.append(finish(2, r2[q], f1_to_2[q]))
    parts = [send(x, 1, 3) for x in parts]
    f2_to_3 = [send(x, 2, 3) for x in f2]
    done = []
    for q in range(n):
        a = after(f2_to_3[q], *[x[0] for x in done])
        done.append(finish(3, r2[q], a, (parts[q], f0[q], f1[q], f2[q])))
    keep = [x for x, _ in done]
    got = [swap(x) for _, x in done]
    return jnp.where(core == 0, jnp.concatenate(keep + got, axis=0), jnp.concatenate(got + keep, axis=0))


def solution(mesh):
    in_specs = (P("rows", None), P("cols", "rows"), P("cols", None, "rows"), P("cols", None, None))
    out_specs = P("rows", "cols")
    return jax.shard_map(
        per_device, mesh=mesh, in_specs=in_specs, out_specs=out_specs, check_vma=False
    )
```

```python
import functools
import math

import jax
import jax.numpy as jnp
from jax import lax
from jax.experimental import pallas as pl
from jax.experimental.pallas import tpu as pltpu
from jax.sharding import PartitionSpec as P

CHUNKS = 2
SIDE = 4
LEAD = 64
SLAB = 32
BF = jnp.bfloat16
F32 = jnp.float32
ANY = pl.BlockSpec(memory_space=pl.ANY)
SMEM = pl.BlockSpec(memory_space=pltpu.SMEM)
VMEM = pl.BlockSpec(memory_space=pltpu.VMEM)


def mm(a, b):
    return jnp.dot(a, b, preferred_element_type=F32)


def after(x, *deps):
    return lax.optimization_barrier((x, *deps))[0]


PIECES = ((0, (0, 1, 2, 3)), (1, (0, 1, 2, 3)), (3, (0, 1, 2, 3)), (2, (0, 1)), (2, (2, 3)))
N_PIECES = 2 * len(PIECES)


def piece_places(info):
    core, y, x = info[1], info[2], info[3]
    for which, parity in ((0, core), (1, 1 - core)):
        for i, (e, along) in enumerate(PIECES):
            for j, d in enumerate(along):
                dy, dx = jnp.where(parity == 0, e, d), jnp.where(parity == 0, d, e)
                yield which * len(PIECES) + i, j, parity, ((y + dy) % SIDE) * SIDE + (x + dx) % SIDE


def start_pieces(info, pieces, r, lv, acc, sems):
    blocks = lv.shape[2] // SLAB
    for i, d, parity, place in piece_places(info):
        pltpu.make_async_copy(pieces[i].at[d], lv.at[parity, place], sems.at[parity]).start()
    copies = [[] for _ in range(2 * blocks)]
    for half in range(2):
        copies[half * blocks].append(pltpu.make_async_copy(r.at[half], acc.at[half], sems.at[2 * blocks + half]))
        copies[half * blocks][0].start()
        copies[half * blocks].append(pltpu.make_async_copy(lv.at[half], lv.at[half], sems.at[half]))
    return copies


def start_diag(info, head, dt_own, dt_oth, gv, dv, sem):
    core = info[1]
    depth = gv.shape[2]
    pltpu.make_async_copy(head.at[:, :, pl.ds(LEAD, depth)], gv, sem.at[0]).start()
    pltpu.make_async_copy(dt_own, dv.at[core], sem.at[1]).start()
    pltpu.make_async_copy(dt_oth, dv.at[1 - core], sem.at[1]).start()


def wait_diag(gv, dv, sem):
    pltpu.make_async_copy(gv, gv, sem.at[0]).wait()
    pltpu.make_async_copy(dv, dv, sem.at[1]).wait()


def solve(running, diag, dt, f):
    size = dt.shape[-1]

    def column(i):
        return running[i // 2, :, (i % 2) * size:(i % 2 + 1) * size]

    def store(i, value):
        f[i // 2, :, (i % 2) * size:(i % 2 + 1) * size] = value

    def left(i, k):
        block = diag[i // 2, :, k * SLAB:(k + 1) * SLAB, (i % 2) * size:(i % 2 + 1) * size]
        return block.reshape(size, size)

    f0 = mm_t(column(0).astype(BF), dt[0, 0]).astype(BF)
    store(0, f0)
    f1 = mm_t((column(1) - mm(f0, left(1, 0))).astype(BF), dt[0, 1]).astype(BF)
    store(1, f1)
    f2 = mm_t((column(2) - mm(f0, left(2, 0)) - mm(f1, left(2, 1))).astype(BF), dt[1, 0]).astype(BF)
    store(2, f2)
    f3 = column(3) - mm(f0, left(3, 0)) - mm(f1, left(3, 1)) - mm(f2, left(3, 2))
    store(3, mm_t(f3.astype(BF), dt[1, 1]).astype(BF))


def hold_kernel(*refs):
    pass


def pick_kernel(info, first, other, out):
    out[...] = jnp.where(info[0] == 1, first[...], other[...])


def scores_kernel(scale, first, info, embeddings, dt_own, dt_oth, head, out, f, emb, lm, gv, dv, sem):
    plane, core = info[0], info[1]
    tokens = embeddings.shape[0] // 2
    ce = pltpu.make_async_copy(embeddings.at[pl.ds(core * tokens + first, emb.shape[0])], emb, sem.at[4])
    ce.start()
    lead = lm.shape[2]
    copies = [pltpu.make_async_copy(head.at[i, :, pl.ds(0, lead)], lm.at[i], sem.at[2 + i]) for i in range(2)]
    for copy in copies:
        copy.start()
    pl.when(plane == 0)(lambda: start_diag(info, head, dt_own, dt_oth, gv, dv, sem))
    ce.wait()
    for half in range(2):
        copies[half].wait()
        points = lm[half].reshape(emb.shape[1], lm.shape[3])
        out[half] = jnp.exp(mm(emb[...], points) * scale)

    @pl.when(plane == 0)
    def _():
        wait_diag(gv, dv, sem)
        solve(out, gv, dv, f)


def start_factor(factor, r, lv, acc, sems):
    depth = lv.shape[2]
    first = factor.shape[2] - depth
    blocks = depth // SLAB
    copies = []
    for half in range(2):
        for k in range(blocks):
            source = factor.at[half, :, pl.ds(first + k * SLAB, SLAB)]
            target = lv.at[half, :, pl.ds(k * SLAB, SLAB)]
            copies.append([pltpu.make_async_copy(source, target, sems.at[half * blocks + k])])
            copies[-1][0].start()
            if k == 0 and r is not None:
                copies[-1].append(pltpu.make_async_copy(r.at[half], acc.at[half], sems.at[2 * blocks + half]))
                copies[-1][1].start()
    return copies


def subtract(acc, a, lv, copies):
    size = lv.shape[1] * SLAB
    blocks = lv.shape[2] // SLAB
    for half in range(2):
        for k in range(blocks):
            for copy in copies[half * blocks + k]:
                copy.wait()
            left = a[k // 2, :, (k % 2) * size:(k % 2 + 1) * size]
            acc[half] -= mm(left, lv[half, :, k * SLAB:(k + 1) * SLAB].reshape(size, -1))


def finish_kernel(role, info, r, a, head, dt_own, dt_oth, *refs):
    last = role == SIDE - 1
    n_factor = N_PIECES if role == 1 else 1
    factor, refs = refs[:n_factor], refs[n_factor:]
    if last:
        part, earlier, (keep, give, f, acc, lv, gv, dv, sems, sem) = refs[0], refs[1:SIDE], refs[SIDE:]
    else:
        f, acc, lv, gv, dv, sems, sem = refs
    plane, core = info[0], info[1]

    @pl.when(plane == role)
    def _():
        if role == 1:
            copies = start_pieces(info, factor, r, lv, acc, sems)
        else:
            copies = start_factor(factor[0], r, lv, acc, sems)
        start_diag(info, head, dt_own, dt_oth, gv, dv, sem)
        subtract(acc, a, lv, copies)
        if last:
            acc[...] += part[...].astype(F32)
        wait_diag(gv, dv, sem)
        solve(acc, gv, dv, f)
        if last:
            keep[...] = f[pl.ds(core, 1)][0]
            give[...] = f[pl.ds(1 - core, 1)][0]

    if last:
        for z, done in enumerate(earlier):

            @pl.when(plane == z)
            def _():
                c0 = pltpu.make_async_copy(done.at[core], keep, sems.at[0])
                c1 = pltpu.make_async_copy(done.at[1 - core], give, sems.at[1])
                c0.start()
                c1.start()
                c0.wait()
                c1.wait()


def partial_kernel(info, factor, own, p, acc, lv, sems):
    @pl.when(info[0] == 1)
    def _():
        copies = start_factor(factor, None, lv, acc, sems)
        acc[...] = jnp.zeros_like(acc)
        subtract(acc, own, lv, copies)
        p[...] = acc[...].astype(BF)


def update_kernel(role, info, r, a, *refs):
    pieces, (r_out, acc, lv, sems) = refs[:N_PIECES], refs[N_PIECES:]

    @pl.when(info[0] == role)
    def _():
        copies = start_pieces(info, pieces, r, lv, acc, sems)
        subtract(acc, a, lv, copies)
        out = pltpu.make_async_copy(acc, r_out, sems.at[0])
        out.start()
        out.wait()


def mm_t(a, b):
    return lax.dot_general(a, b, (((1,), (1,)), ((), ())), preferred_element_type=F32)


def params(mib=60):
    return pltpu.CompilerParams(vmem_limit_bytes=mib << 20)


def cost(us):
    return pl.CostEstimate(flops=int(us * 1e9), bytes_accessed=1 << 10, transcendentals=0)


def per_device(embeddings, landmarks, factor_rows, diag_inverse):
    tokens, depth = embeddings.shape
    rows = lax.axis_size("rows")
    planes = lax.axis_size("cols") // 2
    here = lax.axis_index("cols")
    plane, core = here // 2, here % 2
    row = lax.axis_index("rows")
    own_rows, blocks, slab = factor_rows.shape
    size = diag_inverse.shape[1]
    lead = landmarks.shape[1]
    n = CHUNKS
    half = tokens // 2
    t = half // n
    scale = 0.5 / math.sqrt(depth)
    per_plane = blocks // planes
    info = jnp.stack([plane, core, row // SIDE, row % SIDE]).astype(jnp.int32)

    def send(x, source, target):
        return lax.ppermute(x, "cols", [(2 * source + k, 2 * target + k) for k in range(2)])

    def swap(x):
        return lax.ppermute(x, "cols", [(c, c ^ 1) for c in range(2 * planes)])

    def fetch(x, by, second):
        pairs = []
        for y in range(SIDE):
            for q in range(SIDE):
                for c in range(2, 2 * planes):
                    along_x = (c % 2 == 0) != second
                    sy, sx = (y, (q + by) % SIDE) if along_x else ((y + by) % SIDE, q)
                    pairs.append(((sy * SIDE + sx) * 2 * planes + c, (y * SIDE + q) * 2 * planes + c))
        return lax.ppermute(x, ("rows", "cols"), pairs)

    def hold(x, *deps):
        return pl.pallas_call(
            hold_kernel,
            in_specs=[ANY] * (1 + len(deps)),
            out_specs=ANY,
            out_shape=jax.ShapeDtypeStruct(x.shape, x.dtype),
            input_output_aliases={0: 0},
            cost_estimate=cost(5),
            name="hold",
        )(x, *deps)

    ft = factor_rows.transpose(1, 2, 0)
    groups = [[r * 2 * planes + 2 * z + k for k in range(2) for r in range(rows)] for z in range(planes)]

    def gather(x):
        everyone = lax.all_gather(x, ("rows", "cols"), axis=0, axis_index_groups=groups)
        return everyone.reshape(2, rows, *x.shape)

    diag = lax.dynamic_slice_in_dim(ft, per_plane * plane, per_plane - 1, 0)
    head = gather(jnp.concatenate([landmarks.T, diag.reshape(-1, own_rows)], axis=0))
    dt_own, dt_oth = diag_inverse, swap(diag_inverse)

    near = ft[:per_plane].reshape(-1, own_rows)
    line = jnp.stack([near] + [fetch(near, by, False) for by in range(1, SIDE)])
    up, down = fetch(line, 1, True), fetch(line, 3, True)
    turn = hold(info, line)
    mid = SIDE // 2
    far = [fetch(up[:mid], 1, True), fetch(down[mid:], 3, True)]
    own = [line, up, down]
    oth = [swap(x) for x in own]
    middle = turn = hold(turn, up, down)
    near = own + far + oth + [swap(x) for x in far]
    turn = hold(turn, *far)

    first = send(ft[per_plane:2 * per_plane], 3, 1)
    other = lax.dynamic_slice_in_dim(ft, per_plane * jnp.maximum(plane - 1, 0), per_plane, 0)
    factor = gather(
        pl.pallas_call(
            pick_kernel,
            in_specs=[SMEM, VMEM, VMEM],
            out_specs=VMEM,
            out_shape=jax.ShapeDtypeStruct((per_plane * slab, own_rows), BF),
            cost_estimate=cost(0),
            name="pick",
        )(middle, first.reshape(-1, own_rows), other.reshape(-1, own_rows))
    )

    chunk_f32 = jax.ShapeDtypeStruct((2, t, own_rows), F32)
    chunk_bf = jax.ShapeDtypeStruct((2, t, own_rows), BF)
    whole_bf = jax.ShapeDtypeStruct((2, half, own_rows), BF)
    diag_scratch = [
        pltpu.VMEM((2, rows, (per_plane - 1) * slab, own_rows), BF),
        pltpu.VMEM((2, 2, size, size), BF),
    ]
    factor_scratch = [
        pltpu.VMEM(chunk_f32.shape, F32),
        pltpu.VMEM((2, rows, per_plane * slab, own_rows), BF),
        pltpu.SemaphoreType.DMA((2 * per_plane + 2,)),
    ]
    r, f0 = [], []
    for q in range(n):
        out = pl.pallas_call(
            functools.partial(scores_kernel, scale, q * t),
            in_specs=[SMEM] + [ANY] * 4,
            out_specs=[VMEM] * 2,
            out_shape=[chunk_f32, chunk_bf],
            scratch_shapes=[pltpu.VMEM((t, depth), BF), pltpu.VMEM((2, rows, lead, own_rows), BF)]
            + diag_scratch
            + [pltpu.SemaphoreType.DMA((5,))],
            compiler_params=params(),
            cost_estimate=cost(5),
            name="scores",
        )(turn, after(embeddings, f0[-1]) if q else embeddings, dt_own, dt_oth, head)
        r.append(out[0])
        f0.append(out[1])
    f0_to_1 = [send(x, 0, 1) for x in f0]
    f0_to_3 = [send(x, 0, 3) for x in f0]
    f0_to_2 = [send(x, 3, 2) for x in f0_to_3]
    r[0] = hold(r[0], f0[-1])

    def finish(role, r, a, more=()):
        last = role == planes - 1
        rows_of = near if role == 1 else [factor]
        one = jax.ShapeDtypeStruct((t, own_rows), BF)
        return pl.pallas_call(
            functools.partial(finish_kernel, role),
            in_specs=[SMEM, ANY, VMEM] + [ANY] * (3 + len(rows_of)) + ([VMEM] + [ANY] * 3 if last else []),
            out_specs=[VMEM] * 2 if last else VMEM,
            out_shape=[one, one] if last else chunk_bf,
            scratch_shapes=([pltpu.VMEM(chunk_bf.shape, BF)] if last else [])
            + factor_scratch[:2]
            + diag_scratch
            + [factor_scratch[2], pltpu.SemaphoreType.DMA((2,))],
            compiler_params=params(),
            cost_estimate=cost(0.8),
            name=f"finish{role}",
        )(info, r, a, head, dt_own, dt_oth, *rows_of, *more)

    def partial(own):
        return pl.pallas_call(
            partial_kernel,
            in_specs=[SMEM, ANY, VMEM],
            out_specs=VMEM,
            out_shape=chunk_bf,
            scratch_shapes=factor_scratch,
            compiler_params=params(),
            cost_estimate=cost(0),
            name="partial",
        )(info, factor, own)

    def update(role, r, a):
        return pl.pallas_call(
            functools.partial(update_kernel, role),
            in_specs=[SMEM, ANY, VMEM] + [ANY] * N_PIECES,
            out_specs=ANY,
            out_shape=chunk_f32,
            scratch_shapes=factor_scratch,
            compiler_params=params(),
            cost_estimate=cost(0),
            name="update",
        )(info, r, a, *near)

    f1, parts = [], []
    for q in range(n):
        f1.append(finish(1, r[q], after(f0_to_1[q], *f1)))
    f1_to_2 = [send(x, 1, 2) for x in f1]
    r2, r3, f2 = [], [], []
    for q in range(n):
        r2.append(update(2, r[q], after(f0_to_2[q], f1[-1], *f2)))
        f2.append(finish(2, r2[q], f1_to_2[q]))
        r3.append(update(3, r[q], after(f0_to_3[q], *f2)))
    for i in range(n):
        parts.append(partial(after(f1[i], r2[1], *parts)))
    parts = [send(x, 1, 3) for x in parts]
    f2_to_3 = [send(x, 2, 3) for x in f2]
    done = []
    for q in range(n):
        a = after(f2_to_3[q], *[x[0] for x in done])
        done.append(finish(3, r3[q], a, (parts[q], f0[q], f1[q], f2[q])))
    keep = [x for x, _ in done]
    got = [swap(x) for _, x in done]
    return jnp.where(core == 0, jnp.concatenate(keep + got, axis=0), jnp.concatenate(got + keep, axis=0))


def solution(mesh):
    in_specs = (P("rows", None), P("cols", "rows"), P("cols", None, "rows"), P("cols", None, None))
    out_specs = P("rows", "cols")
    return jax.shard_map(
        per_device, mesh=mesh, in_specs=in_specs, out_specs=out_specs, check_vma=False
    )
```

```python
import functools
import math

import jax
import jax.numpy as jnp
from jax import lax
from jax.experimental import pallas as pl
from jax.experimental.pallas import tpu as pltpu
from jax.sharding import PartitionSpec as P

CHUNKS = 2
SIDE = 4
LEAD = 64
SLAB = 32
BF = jnp.bfloat16
F32 = jnp.float32
ANY = pl.BlockSpec(memory_space=pl.ANY)
SMEM = pl.BlockSpec(memory_space=pltpu.SMEM)
VMEM = pl.BlockSpec(memory_space=pltpu.VMEM)


def mm(a, b):
    return jnp.dot(a, b, preferred_element_type=F32)


def after(x, *deps):
    return lax.optimization_barrier((x, *deps))[0]


PIECES = ((0, (0, 1, 2, 3)), (1, (0, 1, 2, 3)), (3, (0, 1, 2, 3)), (2, (0, 1)), (2, (2, 3)))
N_PIECES = 2 * len(PIECES)


def piece_places(info):
    core, y, x = info[1], info[2], info[3]
    for which, parity in ((0, core), (1, 1 - core)):
        for i, (e, along) in enumerate(PIECES):
            for j, d in enumerate(along):
                dy, dx = jnp.where(parity == 0, e, d), jnp.where(parity == 0, d, e)
                yield which * len(PIECES) + i, j, parity, ((y + dy) % SIDE) * SIDE + (x + dx) % SIDE


def start_pieces(info, pieces, r, lv, acc, sems):
    blocks = lv.shape[2] // SLAB
    for i, d, parity, place in piece_places(info):
        pltpu.make_async_copy(pieces[i].at[d], lv.at[parity, place], sems.at[parity]).start()
    copies = [[] for _ in range(2 * blocks)]
    for half in range(2):
        copies[half * blocks].append(pltpu.make_async_copy(r.at[half], acc.at[half], sems.at[2 * blocks + half]))
        copies[half * blocks][0].start()
        copies[half * blocks].append(pltpu.make_async_copy(lv.at[half], lv.at[half], sems.at[half]))
    return copies


def start_diag(info, head, dt_own, dt_oth, gv, dv, sem):
    core = info[1]
    depth = gv.shape[2]
    pltpu.make_async_copy(head.at[:, :, pl.ds(LEAD, depth)], gv, sem.at[0]).start()
    pltpu.make_async_copy(dt_own, dv.at[core], sem.at[1]).start()
    pltpu.make_async_copy(dt_oth, dv.at[1 - core], sem.at[1]).start()


def wait_diag(gv, dv, sem):
    pltpu.make_async_copy(gv, gv, sem.at[0]).wait()
    pltpu.make_async_copy(dv, dv, sem.at[1]).wait()


def solve(running, diag, dt, f):
    size = dt.shape[-1]

    def column(i):
        return running[i // 2, :, (i % 2) * size:(i % 2 + 1) * size]

    def store(i, value):
        f[i // 2, :, (i % 2) * size:(i % 2 + 1) * size] = value

    def left(i, k):
        block = diag[i // 2, :, k * SLAB:(k + 1) * SLAB, (i % 2) * size:(i % 2 + 1) * size]
        return block.reshape(size, size)

    f0 = mm(column(0).astype(BF), dt[0, 0]).astype(BF)
    store(0, f0)
    f1 = mm((column(1) - mm(f0, left(1, 0))).astype(BF), dt[0, 1]).astype(BF)
    store(1, f1)
    f2 = mm((column(2) - mm(f0, left(2, 0)) - mm(f1, left(2, 1))).astype(BF), dt[1, 0]).astype(BF)
    store(2, f2)
    f3 = column(3) - mm(f0, left(3, 0)) - mm(f1, left(3, 1)) - mm(f2, left(3, 2))
    store(3, mm(f3.astype(BF), dt[1, 1]).astype(BF))


def hold_kernel(*refs):
    pass


def pick_kernel(info, first, other, out):
    out[...] = jnp.where(info[0] == 1, first[...], other[...])


def scores_kernel(scale, info, emb, dt_own, dt_oth, head, out, f, lm, gv, dv, sem):
    plane = info[0]
    lead = lm.shape[2]
    copies = [pltpu.make_async_copy(head.at[i, :, pl.ds(0, lead)], lm.at[i], sem.at[2 + i]) for i in range(2)]
    for copy in copies:
        copy.start()
    pl.when(plane == 0)(lambda: start_diag(info, head, dt_own, dt_oth, gv, dv, sem))
    for half in range(2):
        copies[half].wait()
        points = lm[half].reshape(emb.shape[1], lm.shape[3])
        out[half] = jnp.exp(mm(emb[...], points) * scale)

    @pl.when(plane == 0)
    def _():
        wait_diag(gv, dv, sem)
        solve(out, gv, dv, f)


def start_factor(factor, r, lv, acc, sems):
    depth = lv.shape[2]
    first = factor.shape[2] - depth
    blocks = depth // SLAB
    copies = []
    for half in range(2):
        for k in range(blocks):
            source = factor.at[half, :, pl.ds(first + k * SLAB, SLAB)]
            target = lv.at[half, :, pl.ds(k * SLAB, SLAB)]
            copies.append([pltpu.make_async_copy(source, target, sems.at[half * blocks + k])])
            copies[-1][0].start()
            if k == 0 and r is not None:
                copies[-1].append(pltpu.make_async_copy(r.at[half], acc.at[half], sems.at[2 * blocks + half]))
                copies[-1][1].start()
    return copies


def subtract(acc, a, lv, copies):
    size = lv.shape[1] * SLAB
    blocks = lv.shape[2] // SLAB
    for half in range(2):
        for k in range(blocks):
            for copy in copies[half * blocks + k]:
                copy.wait()
            left = a[k // 2, :, (k % 2) * size:(k % 2 + 1) * size]
            acc[half] -= mm(left, lv[half, :, k * SLAB:(k + 1) * SLAB].reshape(size, -1))


def finish_kernel(role, info, r, a, head, dt_own, dt_oth, *refs):
    last = role == SIDE - 1
    n_factor = N_PIECES if role == 1 else 1
    factor, refs = refs[:n_factor], refs[n_factor:]
    if last:
        part, earlier, (keep, give, f, acc, lv, gv, dv, sems, sem) = refs[0], refs[1:SIDE], refs[SIDE:]
    else:
        f, acc, lv, gv, dv, sems, sem = refs
    plane, core = info[0], info[1]

    @pl.when(plane == role)
    def _():
        if role == 1:
            copies = start_pieces(info, factor, r, lv, acc, sems)
        else:
            copies = start_factor(factor[0], r, lv, acc, sems)
        start_diag(info, head, dt_own, dt_oth, gv, dv, sem)
        subtract(acc, a, lv, copies)
        if last:
            acc[...] += part[...].astype(F32)
        wait_diag(gv, dv, sem)
        solve(acc, gv, dv, f)
        if last:
            keep[...] = f[pl.ds(core, 1)][0]
            give[...] = f[pl.ds(1 - core, 1)][0]

    if last:
        for z, done in enumerate(earlier):

            @pl.when(plane == z)
            def _():
                c0 = pltpu.make_async_copy(done.at[core], keep, sems.at[0])
                c1 = pltpu.make_async_copy(done.at[1 - core], give, sems.at[1])
                c0.start()
                c1.start()
                c0.wait()
                c1.wait()


def partial_kernel(info, factor, own, p, acc, lv, sems):
    @pl.when(info[0] == 1)
    def _():
        copies = start_factor(factor, None, lv, acc, sems)
        acc[...] = jnp.zeros_like(acc)
        subtract(acc, own, lv, copies)
        p[...] = acc[...].astype(BF)


def update_kernel(role, info, r, a, *refs):
    pieces, (r_out, acc, lv, sems) = refs[:N_PIECES], refs[N_PIECES:]

    @pl.when(info[0] == role)
    def _():
        copies = start_pieces(info, pieces, r, lv, acc, sems)
        subtract(acc, a, lv, copies)
        out = pltpu.make_async_copy(acc, r_out, sems.at[0])
        out.start()
        out.wait()


def params(mib=60):
    return pltpu.CompilerParams(vmem_limit_bytes=mib << 20)


def cost(us):
    return pl.CostEstimate(flops=int(us * 1e9), bytes_accessed=1 << 10, transcendentals=0)


def per_device(embeddings, landmarks, factor_rows, diag_inverse):
    tokens, depth = embeddings.shape
    rows = lax.axis_size("rows")
    planes = lax.axis_size("cols") // 2
    here = lax.axis_index("cols")
    plane, core = here // 2, here % 2
    row = lax.axis_index("rows")
    own_rows, blocks, slab = factor_rows.shape
    size = diag_inverse.shape[1]
    lead = landmarks.shape[1]
    n = CHUNKS
    half = tokens // 2
    t = half // n
    scale = 0.5 / math.sqrt(depth)
    per_plane = blocks // planes
    info = jnp.stack([plane, core, row // SIDE, row % SIDE]).astype(jnp.int32)

    def send(x, source, target):
        return lax.ppermute(x, "cols", [(2 * source + k, 2 * target + k) for k in range(2)])

    def swap(x):
        return lax.ppermute(x, "cols", [(c, c ^ 1) for c in range(2 * planes)])

    def fetch(x, by, second):
        pairs = []
        for y in range(SIDE):
            for q in range(SIDE):
                for c in range(2, 2 * planes):
                    along_x = (c % 2 == 0) != second
                    sy, sx = (y, (q + by) % SIDE) if along_x else ((y + by) % SIDE, q)
                    pairs.append(((sy * SIDE + sx) * 2 * planes + c, (y * SIDE + q) * 2 * planes + c))
        return lax.ppermute(x, ("rows", "cols"), pairs)

    def hold(x, *deps):
        return pl.pallas_call(
            hold_kernel,
            in_specs=[ANY] * (1 + len(deps)),
            out_specs=ANY,
            out_shape=jax.ShapeDtypeStruct(x.shape, x.dtype),
            input_output_aliases={0: 0},
            cost_estimate=cost(5),
            name="hold",
        )(x, *deps)

    ft = factor_rows.transpose(1, 2, 0)
    groups = [[r * 2 * planes + 2 * z + k for k in range(2) for r in range(rows)] for z in range(planes)]

    def gather(x):
        everyone = lax.all_gather(x, ("rows", "cols"), axis=0, axis_index_groups=groups)
        return everyone.reshape(2, rows, *x.shape)

    diag = lax.dynamic_slice_in_dim(ft, per_plane * plane, per_plane - 1, 0)
    head = gather(jnp.concatenate([landmarks.T, diag.reshape(-1, own_rows)], axis=0))
    dt_own = diag_inverse.transpose(0, 2, 1)
    dt_oth = swap(dt_own)

    near = ft[:per_plane].reshape(-1, own_rows)
    line = jnp.stack([near] + [fetch(near, by, False) for by in range(1, SIDE)])
    up, down = fetch(line, 1, True), fetch(line, 3, True)
    turn = hold(info, line)
    mid = SIDE // 2
    far = [fetch(up[:mid], 1, True), fetch(down[mid:], 3, True)]
    own = [line, up, down]
    oth = [swap(x) for x in own]
    middle = turn = hold(turn, up, down)
    near = own + far + oth + [swap(x) for x in far]
    turn = hold(turn, *far)

    first = send(ft[per_plane:2 * per_plane], 3, 1)
    other = lax.dynamic_slice_in_dim(ft, per_plane * jnp.maximum(plane - 1, 0), per_plane, 0)
    factor = gather(
        pl.pallas_call(
            pick_kernel,
            in_specs=[SMEM, VMEM, VMEM],
            out_specs=VMEM,
            out_shape=jax.ShapeDtypeStruct((per_plane * slab, own_rows), BF),
            cost_estimate=cost(0),
            name="pick",
        )(middle, first.reshape(-1, own_rows), other.reshape(-1, own_rows))
    )

    emb = lax.dynamic_slice_in_dim(embeddings, core * half, half, 0)
    chunk_f32 = jax.ShapeDtypeStruct((2, t, own_rows), F32)
    chunk_bf = jax.ShapeDtypeStruct((2, t, own_rows), BF)
    whole_bf = jax.ShapeDtypeStruct((2, half, own_rows), BF)
    diag_scratch = [
        pltpu.VMEM((2, rows, (per_plane - 1) * slab, own_rows), BF),
        pltpu.VMEM((2, 2, size, size), BF),
    ]
    factor_scratch = [
        pltpu.VMEM(chunk_f32.shape, F32),
        pltpu.VMEM((2, rows, per_plane * slab, own_rows), BF),
        pltpu.SemaphoreType.DMA((2 * per_plane + 2,)),
    ]
    r, f0 = [], []
    for q in range(n):
        x = emb[q * t:(q + 1) * t]
        out = pl.pallas_call(
            functools.partial(scores_kernel, scale),
            in_specs=[SMEM, VMEM] + [ANY] * 3,
            out_specs=[VMEM] * 2,
            out_shape=[chunk_f32, chunk_bf],
            scratch_shapes=[pltpu.VMEM((2, rows, lead, own_rows), BF)]
            + diag_scratch
            + [pltpu.SemaphoreType.DMA((4,))],
            compiler_params=params(),
            cost_estimate=cost(5),
            name="scores",
        )(turn, after(x, f0[-1]) if q else x, dt_own, dt_oth, head)
        r.append(out[0])
        f0.append(out[1])
    f0_to_1 = [send(x, 0, 1) for x in f0]
    f0_to_3 = [send(x, 0, 3) for x in f0]
    f0_to_2 = [send(x, 3, 2) for x in f0_to_3]
    r[0] = hold(r[0], f0[-1])

    def finish(role, r, a, more=()):
        last = role == planes - 1
        rows_of = near if role == 1 else [factor]
        one = jax.ShapeDtypeStruct((t, own_rows), BF)
        return pl.pallas_call(
            functools.partial(finish_kernel, role),
            in_specs=[SMEM, ANY, VMEM] + [ANY] * (3 + len(rows_of)) + ([VMEM] + [ANY] * 3 if last else []),
            out_specs=[VMEM] * 2 if last else VMEM,
            out_shape=[one, one] if last else chunk_bf,
            scratch_shapes=([pltpu.VMEM(chunk_bf.shape, BF)] if last else [])
            + factor_scratch[:2]
            + diag_scratch
            + [factor_scratch[2], pltpu.SemaphoreType.DMA((2,))],
            compiler_params=params(),
            cost_estimate=cost(0.8),
            name=f"finish{role}",
        )(info, r, a, head, dt_own, dt_oth, *rows_of, *more)

    def partial(own):
        return pl.pallas_call(
            partial_kernel,
            in_specs=[SMEM, ANY, VMEM],
            out_specs=VMEM,
            out_shape=chunk_bf,
            scratch_shapes=factor_scratch,
            compiler_params=params(),
            cost_estimate=cost(0),
            name="partial",
        )(info, factor, own)

    def update(role, r, a):
        return pl.pallas_call(
            functools.partial(update_kernel, role),
            in_specs=[SMEM, ANY, VMEM] + [ANY] * N_PIECES,
            out_specs=ANY,
            out_shape=chunk_f32,
            scratch_shapes=factor_scratch,
            compiler_params=params(),
            cost_estimate=cost(0),
            name="update",
        )(info, r, a, *near)

    f1, parts = [], []
    for q in range(n):
        f1.append(finish(1, r[q], after(f0_to_1[q], *f1)))
    f1_to_2 = [send(x, 1, 2) for x in f1]
    r2, r3, f2 = [], [], []
    for q in range(n):
        r2.append(update(2, r[q], after(f0_to_2[q], f1[-1], *f2)))
        f2.append(finish(2, r2[q], f1_to_2[q]))
        r3.append(update(3, r[q], after(f0_to_3[q], *f2)))
    for i in range(n):
        parts.append(partial(after(f1[i], r2[1], *parts)))
    parts = [send(x, 1, 3) for x in parts]
    f2_to_3 = [send(x, 2, 3) for x in f2]
    done = []
    for q in range(n):
        a = after(f2_to_3[q], *[x[0] for x in done])
        done.append(finish(3, r3[q], a, (parts[q], f0[q], f1[q], f2[q])))
    keep = [x for x, _ in done]
    got = [swap(x) for _, x in done]
    return jnp.where(core == 0, jnp.concatenate(keep + got, axis=0), jnp.concatenate(got + keep, axis=0))


def solution(mesh):
    in_specs = (P("rows", None), P("cols", "rows"), P("cols", None, "rows"), P("cols", None, None))
    out_specs = P("rows", "cols")
    return jax.shard_map(
        per_device, mesh=mesh, in_specs=in_specs, out_specs=out_specs, check_vma=False
    )
```

```python
import functools
import math

import jax
import jax.numpy as jnp
from jax import lax
from jax.experimental import pallas as pl
from jax.experimental.pallas import tpu as pltpu
from jax.sharding import PartitionSpec as P

CHUNKS = 2
SIDE = 4
LEAD = 64
SLAB = 32
BF = jnp.bfloat16
F32 = jnp.float32
ANY = pl.BlockSpec(memory_space=pl.ANY)
SMEM = pl.BlockSpec(memory_space=pltpu.SMEM)
VMEM = pl.BlockSpec(memory_space=pltpu.VMEM)


def mm(a, b):
    return jnp.dot(a, b, preferred_element_type=F32)


def after(x, *deps):
    return lax.optimization_barrier((x, *deps))[0]


PIECES = ((0, (0, 1, 2, 3)), (1, (0, 1, 2, 3)), (3, (0, 1, 2, 3)), (2, (0, 1)), (2, (2, 3)))
N_PIECES = 2 * len(PIECES)


def piece_places(info):
    core, y, x = info[1], info[2], info[3]
    for which, parity in ((0, core), (1, 1 - core)):
        for i, (e, along) in enumerate(PIECES):
            for j, d in enumerate(along):
                dy, dx = jnp.where(parity == 0, e, d), jnp.where(parity == 0, d, e)
                yield which * len(PIECES) + i, j, parity, ((y + dy) % SIDE) * SIDE + (x + dx) % SIDE


def start_pieces(info, pieces, r, lv, acc, sems):
    blocks = lv.shape[2] // SLAB
    for i, d, parity, place in piece_places(info):
        pltpu.make_async_copy(pieces[i].at[d], lv.at[parity, place], sems.at[parity]).start()
    copies = [[] for _ in range(2 * blocks)]
    for half in range(2):
        copies[half * blocks].append(pltpu.make_async_copy(r.at[half], acc.at[half], sems.at[2 * blocks + half]))
        copies[half * blocks][0].start()
        copies[half * blocks].append(pltpu.make_async_copy(lv.at[half], lv.at[half], sems.at[half]))
    return copies


def start_diag(info, head, dt_own, dt_oth, gv, dv, sem):
    core = info[1]
    depth = gv.shape[2]
    pltpu.make_async_copy(head.at[:, :, pl.ds(LEAD, depth)], gv, sem.at[0]).start()
    pltpu.make_async_copy(dt_own, dv.at[core], sem.at[1]).start()
    pltpu.make_async_copy(dt_oth, dv.at[1 - core], sem.at[1]).start()


def wait_diag(gv, dv, sem):
    pltpu.make_async_copy(gv, gv, sem.at[0]).wait()
    pltpu.make_async_copy(dv, dv, sem.at[1]).wait()


def solve(running, diag, dt, f):
    size = dt.shape[-1]

    def column(i):
        return running[i // 2, :, (i % 2) * size:(i % 2 + 1) * size]

    def store(i, value):
        f[i // 2, :, (i % 2) * size:(i % 2 + 1) * size] = value

    def left(i, k):
        block = diag[i // 2, :, k * SLAB:(k + 1) * SLAB, (i % 2) * size:(i % 2 + 1) * size]
        return block.reshape(size, size)

    f0 = mm_t(column(0).astype(BF), dt[0, 0]).astype(BF)
    store(0, f0)
    f1 = mm_t((column(1) - mm(f0, left(1, 0))).astype(BF), dt[0, 1]).astype(BF)
    store(1, f1)
    f2 = mm_t((column(2) - mm(f0, left(2, 0)) - mm(f1, left(2, 1))).astype(BF), dt[1, 0]).astype(BF)
    store(2, f2)
    f3 = column(3) - mm(f0, left(3, 0)) - mm(f1, left(3, 1)) - mm(f2, left(3, 2))
    store(3, mm_t(f3.astype(BF), dt[1, 1]).astype(BF))


def hold_kernel(*refs):
    pass


def pick_kernel(info, first, other, out):
    out[...] = jnp.where(info[0] == 1, first[...], other[...])


def scores_kernel(scale, first, info, embeddings, dt_own, dt_oth, head, out, f, emb, lm, gv, dv, sem):
    plane, core = info[0], info[1]
    tokens = embeddings.shape[0] // 2
    ce = pltpu.make_async_copy(embeddings.at[pl.ds(core * tokens + first, emb.shape[0])], emb, sem.at[4])
    ce.start()
    lead = lm.shape[2]
    copies = [pltpu.make_async_copy(head.at[i, :, pl.ds(0, lead)], lm.at[i], sem.at[2 + i]) for i in range(2)]
    for copy in copies:
        copy.start()
    pl.when(plane == 0)(lambda: start_diag(info, head, dt_own, dt_oth, gv, dv, sem))
    ce.wait()
    for half in range(2):
        copies[half].wait()
        points = lm[half].reshape(emb.shape[1], lm.shape[3])
        out[half] = jnp.exp(mm(emb[...], points) * scale)

    @pl.when(plane == 0)
    def _():
        wait_diag(gv, dv, sem)
        solve(out, gv, dv, f)


def start_factor(factor, r, lv, acc, sems):
    depth = lv.shape[2]
    first = factor.shape[2] - depth
    blocks = depth // SLAB
    copies = []
    for half in range(2):
        for k in range(blocks):
            source = factor.at[half, :, pl.ds(first + k * SLAB, SLAB)]
            target = lv.at[half, :, pl.ds(k * SLAB, SLAB)]
            copies.append([pltpu.make_async_copy(source, target, sems.at[half * blocks + k])])
            copies[-1][0].start()
            if k == 0 and r is not None:
                copies[-1].append(pltpu.make_async_copy(r.at[half], acc.at[half], sems.at[2 * blocks + half]))
                copies[-1][1].start()
    return copies


def subtract(acc, a, lv, copies):
    size = lv.shape[1] * SLAB
    blocks = lv.shape[2] // SLAB
    for half in range(2):
        for k in range(blocks):
            for copy in copies[half * blocks + k]:
                copy.wait()
            left = a[k // 2, :, (k % 2) * size:(k % 2 + 1) * size]
            acc[half] -= mm(left, lv[half, :, k * SLAB:(k + 1) * SLAB].reshape(size, -1))


def finish_kernel(role, info, r, a, head, dt_own, dt_oth, *refs):
    last = role == SIDE - 1
    n_factor = N_PIECES if role == 1 else 1
    factor, refs = refs[:n_factor], refs[n_factor:]
    if last:
        part, earlier, (keep, give, f, acc, lv, gv, dv, sems, sem) = refs[0], refs[1:SIDE], refs[SIDE:]
    else:
        f, acc, lv, gv, dv, sems, sem = refs
    plane, core = info[0], info[1]

    @pl.when(plane == role)
    def _():
        if role == 1:
            copies = start_pieces(info, factor, r, lv, acc, sems)
        else:
            copies = start_factor(factor[0], r, lv, acc, sems)
        start_diag(info, head, dt_own, dt_oth, gv, dv, sem)
        subtract(acc, a, lv, copies)
        if last:
            acc[...] += part[...].astype(F32)
        wait_diag(gv, dv, sem)
        solve(acc, gv, dv, f)
        if last:
            keep[...] = f[pl.ds(core, 1)][0]
            give[...] = f[pl.ds(1 - core, 1)][0]

    if last:
        for z, done in enumerate(earlier):

            @pl.when(plane == z)
            def _():
                c0 = pltpu.make_async_copy(done.at[core], keep, sems.at[0])
                c1 = pltpu.make_async_copy(done.at[1 - core], give, sems.at[1])
                c0.start()
                c1.start()
                c0.wait()
                c1.wait()


def partial_kernel(info, factor, own, p, acc, lv, sems):
    @pl.when(info[0] == 1)
    def _():
        copies = start_factor(factor, None, lv, acc, sems)
        acc[...] = jnp.zeros_like(acc)
        subtract(acc, own, lv, copies)
        p[...] = acc[...].astype(BF)


def update_kernel(info, r, to_3, to_2, *refs):
    pieces, (r_out, acc, lv, av, sems, sem) = refs[:N_PIECES], refs[N_PIECES:]

    @pl.when(info[0] >= 2)
    def _():
        for plane, a in ((2, to_2), (3, to_3)):
            pl.when(info[0] == plane)(lambda a=a: pltpu.make_async_copy(a, av, sem).start())
        copies = start_pieces(info, pieces, r, lv, acc, sems)
        pltpu.make_async_copy(to_2, av, sem).wait()
        subtract(acc, av, lv, copies)
        out = pltpu.make_async_copy(acc, r_out, sem)
        out.start()
        out.wait()


def mm_t(a, b):
    return lax.dot_general(a, b, (((1,), (1,)), ((), ())), preferred_element_type=F32)


def params(mib=60):
    return pltpu.CompilerParams(vmem_limit_bytes=mib << 20)


def cost(us):
    return pl.CostEstimate(flops=int(us * 1e9), bytes_accessed=1 << 10, transcendentals=0)


def per_device(embeddings, landmarks, factor_rows, diag_inverse):
    tokens, depth = embeddings.shape
    rows = lax.axis_size("rows")
    planes = lax.axis_size("cols") // 2
    here = lax.axis_index("cols")
    plane, core = here // 2, here % 2
    row = lax.axis_index("rows")
    own_rows, blocks, slab = factor_rows.shape
    size = diag_inverse.shape[1]
    lead = landmarks.shape[1]
    n = CHUNKS
    half = tokens // 2
    t = half // n
    scale = 0.5 / math.sqrt(depth)
    per_plane = blocks // planes
    info = jnp.stack([plane, core, row // SIDE, row % SIDE]).astype(jnp.int32)

    def send(x, source, target):
        return lax.ppermute(x, "cols", [(2 * source + k, 2 * target + k) for k in range(2)])

    def swap(x):
        return lax.ppermute(x, "cols", [(c, c ^ 1) for c in range(2 * planes)])

    def fetch(x, by, second):
        pairs = []
        for y in range(SIDE):
            for q in range(SIDE):
                for c in range(2, 2 * planes):
                    along_x = (c % 2 == 0) != second
                    sy, sx = (y, (q + by) % SIDE) if along_x else ((y + by) % SIDE, q)
                    pairs.append(((sy * SIDE + sx) * 2 * planes + c, (y * SIDE + q) * 2 * planes + c))
        return lax.ppermute(x, ("rows", "cols"), pairs)

    def hold(x, *deps):
        return pl.pallas_call(
            hold_kernel,
            in_specs=[ANY] * (1 + len(deps)),
            out_specs=ANY,
            out_shape=jax.ShapeDtypeStruct(x.shape, x.dtype),
            input_output_aliases={0: 0},
            cost_estimate=cost(5),
            name="hold",
        )(x, *deps)

    ft = factor_rows.transpose(1, 2, 0)
    groups = [[r * 2 * planes + 2 * z + k for k in range(2) for r in range(rows)] for z in range(planes)]

    def gather(x):
        everyone = lax.all_gather(x, ("rows", "cols"), axis=0, axis_index_groups=groups)
        return everyone.reshape(2, rows, *x.shape)

    diag = lax.dynamic_slice_in_dim(ft, per_plane * plane, per_plane - 1, 0)
    head = gather(jnp.concatenate([landmarks.T, diag.reshape(-1, own_rows)], axis=0))
    dt_own, dt_oth = diag_inverse, swap(diag_inverse)

    near = ft[:per_plane].reshape(-1, own_rows)
    line = jnp.stack([near] + [fetch(near, by, False) for by in range(1, SIDE)])
    up, down = fetch(line, 1, True), fetch(line, 3, True)
    turn = hold(info, line)
    mid = SIDE // 2
    far = [fetch(up[:mid], 1, True), fetch(down[mid:], 3, True)]
    own = [line, up, down]
    oth = [swap(x) for x in own]
    middle = turn = hold(turn, up, down)
    near = own + far + oth + [swap(x) for x in far]
    turn = hold(turn, *far)

    first = send(ft[per_plane:2 * per_plane], 3, 1)
    other = lax.dynamic_slice_in_dim(ft, per_plane * jnp.maximum(plane - 1, 0), per_plane, 0)
    factor = gather(
        pl.pallas_call(
            pick_kernel,
            in_specs=[SMEM, VMEM, VMEM],
            out_specs=VMEM,
            out_shape=jax.ShapeDtypeStruct((per_plane * slab, own_rows), BF),
            cost_estimate=cost(0),
            name="pick",
        )(middle, first.reshape(-1, own_rows), other.reshape(-1, own_rows))
    )

    chunk_f32 = jax.ShapeDtypeStruct((2, t, own_rows), F32)
    chunk_bf = jax.ShapeDtypeStruct((2, t, own_rows), BF)
    whole_bf = jax.ShapeDtypeStruct((2, half, own_rows), BF)
    diag_scratch = [
        pltpu.VMEM((2, rows, (per_plane - 1) * slab, own_rows), BF),
        pltpu.VMEM((2, 2, size, size), BF),
    ]
    factor_scratch = [
        pltpu.VMEM(chunk_f32.shape, F32),
        pltpu.VMEM((2, rows, per_plane * slab, own_rows), BF),
        pltpu.SemaphoreType.DMA((2 * per_plane + 2,)),
    ]
    r, f0 = [], []
    for q in range(n):
        out = pl.pallas_call(
            functools.partial(scores_kernel, scale, q * t),
            in_specs=[SMEM] + [ANY] * 4,
            out_specs=[VMEM] * 2,
            out_shape=[chunk_f32, chunk_bf],
            scratch_shapes=[pltpu.VMEM((t, depth), BF), pltpu.VMEM((2, rows, lead, own_rows), BF)]
            + diag_scratch
            + [pltpu.SemaphoreType.DMA((5,))],
            compiler_params=params(),
            cost_estimate=cost(5),
            name="scores",
        )(turn, after(embeddings, f0[-1]) if q else embeddings, dt_own, dt_oth, head)
        r.append(out[0])
        f0.append(out[1])
    f0_to_1 = [send(x, 0, 1) for x in f0]
    f0_to_3 = [send(x, 0, 3) for x in f0]
    f0_to_2 = [send(x, 3, 2) for x in f0_to_3]
    r[0] = hold(r[0], f0[-1])

    def finish(role, r, a, more=()):
        last = role == planes - 1
        rows_of = near if role == 1 else [factor]
        one = jax.ShapeDtypeStruct((t, own_rows), BF)
        return pl.pallas_call(
            functools.partial(finish_kernel, role),
            in_specs=[SMEM, ANY, VMEM] + [ANY] * (3 + len(rows_of)) + ([VMEM] + [ANY] * 3 if last else []),
            out_specs=[VMEM] * 2 if last else VMEM,
            out_shape=[one, one] if last else chunk_bf,
            scratch_shapes=([pltpu.VMEM(chunk_bf.shape, BF)] if last else [])
            + factor_scratch[:2]
            + diag_scratch
            + [factor_scratch[2], pltpu.SemaphoreType.DMA((2,))],
            compiler_params=params(),
            cost_estimate=cost(0.8),
            name=f"finish{role}",
        )(info, r, a, head, dt_own, dt_oth, *rows_of, *more)

    def partial(own):
        return pl.pallas_call(
            partial_kernel,
            in_specs=[SMEM, ANY, VMEM],
            out_specs=VMEM,
            out_shape=chunk_bf,
            scratch_shapes=factor_scratch,
            compiler_params=params(),
            cost_estimate=cost(0),
            name="partial",
        )(info, factor, own)

    def update(r, to_3, to_2):
        return pl.pallas_call(
            update_kernel,
            in_specs=[SMEM] + [ANY] * (3 + N_PIECES),
            out_specs=ANY,
            out_shape=chunk_f32,
            scratch_shapes=factor_scratch[:2]
            + [pltpu.VMEM(chunk_bf.shape, BF), factor_scratch[2], pltpu.SemaphoreType.DMA],
            compiler_params=params(),
            cost_estimate=cost(0),
            name="update",
        )(info, r, to_3, to_2, *near)

    f1, parts = [], []
    for q in range(n):
        f1.append(finish(1, r[q], after(f0_to_1[q], *f1)))
    f1_to_2 = [send(x, 1, 2) for x in f1]
    r2, f2 = [], []
    for q in range(n):
        r2.append(update(r[q], f0_to_3[q], after(f0_to_2[q], f1[-1], *f2)))
        f2.append(finish(2, r2[q], f1_to_2[q]))
    for i in range(n):
        parts.append(partial(after(f1[i], r2[1], *parts)))
    parts = [send(x, 1, 3) for x in parts]
    f2_to_3 = [send(x, 2, 3) for x in f2]
    done = []
    for q in range(n):
        a = after(f2_to_3[q], *[x[0] for x in done])
        done.append(finish(3, r2[q], a, (parts[q], f0[q], f1[q], f2[q])))
    keep = [x for x, _ in done]
    got = [swap(x) for _, x in done]
    return jnp.where(core == 0, jnp.concatenate(keep + got, axis=0), jnp.concatenate(got + keep, axis=0))


def solution(mesh):
    in_specs = (P("rows", None), P("cols", "rows"), P("cols", None, "rows"), P("cols", None, None))
    out_specs = P("rows", "cols")
    return jax.shard_map(
        per_device, mesh=mesh, in_specs=in_specs, out_specs=out_specs, check_vma=False
    )
```

```python
import functools
import math

import jax
import jax.numpy as jnp
from jax import lax
from jax.experimental import pallas as pl
from jax.experimental.pallas import tpu as pltpu
from jax.sharding import PartitionSpec as P

CHUNKS = 2
SIDE = 4
LEAD = 64
SLAB = 32
BF = jnp.bfloat16
F32 = jnp.float32
ANY = pl.BlockSpec(memory_space=pl.ANY)
SMEM = pl.BlockSpec(memory_space=pltpu.SMEM)
VMEM = pl.BlockSpec(memory_space=pltpu.VMEM)


def mm(a, b):
    return jnp.dot(a, b, preferred_element_type=F32)


def after(x, *deps):
    return lax.optimization_barrier((x, *deps))[0]


PIECES = ((0, (0, 1, 2, 3)), (1, (0, 1, 2, 3)), (3, (0, 1, 2, 3)), (2, (0, 1)), (2, (2, 3)))
N_PIECES = 2 * len(PIECES)


def piece_places(info):
    core, y, x = info[1], info[2], info[3]
    for which, parity in ((0, core), (1, 1 - core)):
        for i, (e, along) in enumerate(PIECES):
            for j, d in enumerate(along):
                dy, dx = jnp.where(parity == 0, e, d), jnp.where(parity == 0, d, e)
                yield which * len(PIECES) + i, j, parity, ((y + dy) % SIDE) * SIDE + (x + dx) % SIDE


def halves(info):
    return enumerate((info[1], 1 - info[1]))


def start_pieces(info, pieces, r, lv, acc, sems):
    blocks = lv.shape[2] // SLAB
    for i, half in halves(info):
        pltpu.make_async_copy(r.at[half], acc.at[half], sems.at[2 * blocks + i]).start()
    for i, d, parity, place in piece_places(info):
        pltpu.make_async_copy(pieces[i].at[d], lv.at[parity, place], sems.at[i // len(PIECES)]).start()

    def wait(i, half, k):
        if k == 0:
            pltpu.make_async_copy(lv.at[half], lv.at[half], sems.at[i]).wait()
            pltpu.make_async_copy(acc.at[half], acc.at[half], sems.at[2 * blocks + i]).wait()

    return wait


def start_diag(info, head, dt_own, dt_oth, gv, dv, sem):
    core = info[1]
    depth = gv.shape[2]
    pltpu.make_async_copy(head.at[:, :, pl.ds(LEAD, depth)], gv, sem.at[0]).start()
    pltpu.make_async_copy(dt_own, dv.at[core], sem.at[1]).start()
    pltpu.make_async_copy(dt_oth, dv.at[1 - core], sem.at[1]).start()


def wait_diag(gv, dv, sem):
    pltpu.make_async_copy(gv, gv, sem.at[0]).wait()
    pltpu.make_async_copy(dv, dv, sem.at[1]).wait()


def solve(running, diag, dt, f):
    size = dt.shape[-1]

    def column(i):
        return running[i // 2, :, (i % 2) * size:(i % 2 + 1) * size]

    def store(i, value):
        f[i // 2, :, (i % 2) * size:(i % 2 + 1) * size] = value

    def left(i, k):
        block = diag[i // 2, :, k * SLAB:(k + 1) * SLAB, (i % 2) * size:(i % 2 + 1) * size]
        return block.reshape(size, size)

    f0 = mm_t(column(0).astype(BF), dt[0, 0]).astype(BF)
    store(0, f0)
    f1 = mm_t((column(1) - mm(f0, left(1, 0))).astype(BF), dt[0, 1]).astype(BF)
    store(1, f1)
    f2 = mm_t((column(2) - mm(f0, left(2, 0)) - mm(f1, left(2, 1))).astype(BF), dt[1, 0]).astype(BF)
    store(2, f2)
    f3 = column(3) - mm(f0, left(3, 0)) - mm(f1, left(3, 1)) - mm(f2, left(3, 2))
    store(3, mm_t(f3.astype(BF), dt[1, 1]).astype(BF))


def hold_kernel(*refs):
    pass


def pick_kernel(info, first, other, out):
    out[...] = jnp.where(info[0] == 1, first[...], other[...])


def scores_kernel(scale, first, info, embeddings, dt_own, dt_oth, head, out, f, emb, lm, gv, dv, sem):
    plane, core = info[0], info[1]
    tokens = embeddings.shape[0] // 2
    ce = pltpu.make_async_copy(embeddings.at[pl.ds(core * tokens + first, emb.shape[0])], emb, sem.at[4])
    ce.start()
    lead = lm.shape[2]
    copies = [pltpu.make_async_copy(head.at[i, :, pl.ds(0, lead)], lm.at[i], sem.at[2 + i]) for i in range(2)]
    for copy in copies:
        copy.start()
    pl.when(plane == 0)(lambda: start_diag(info, head, dt_own, dt_oth, gv, dv, sem))
    ce.wait()
    for half in range(2):
        copies[half].wait()
        points = lm[half].reshape(emb.shape[1], lm.shape[3])
        out[half] = jnp.exp(mm(emb[...], points) * scale)

    @pl.when(plane == 0)
    def _():
        wait_diag(gv, dv, sem)
        solve(out, gv, dv, f)


def start_factor(info, factor, r, lv, acc, sems):
    blocks = lv.shape[2] // SLAB

    def block(ref, half, k):
        return ref.at[half, :, pl.ds(k * SLAB, SLAB)]

    for i, half in halves(info):
        for k in range(blocks):
            pltpu.make_async_copy(block(factor, half, k), block(lv, half, k), sems.at[i * blocks + k]).start()
            if k == 0 and r is not None:
                pltpu.make_async_copy(r.at[half], acc.at[half], sems.at[2 * blocks + i]).start()

    def wait(i, half, k):
        pltpu.make_async_copy(block(lv, half, k), block(lv, half, k), sems.at[i * blocks + k]).wait()
        if k == 0 and r is not None:
            pltpu.make_async_copy(acc.at[half], acc.at[half], sems.at[2 * blocks + i]).wait()

    return wait


def subtract(info, acc, a, lv, wait):
    size = lv.shape[1] * SLAB

    def body(i, carry):
        half = jnp.where(i == 0, info[1], 1 - info[1])
        for k in range(lv.shape[2] // SLAB):
            wait(i, half, k)
            left = a[k // 2, :, (k % 2) * size:(k % 2 + 1) * size]
            acc[half] = acc[half] - mm(left, lv[half, :, k * SLAB:(k + 1) * SLAB].reshape(size, -1))
        return carry

    lax.fori_loop(0, 2, body, 0)


def both_kernel(info, r, a, head, dt_own, dt_oth, factor, before, *refs):
    pieces, (f, acc, lv, gv, dv, sems, sem, near, near_sems) = refs[:N_PIECES], refs[N_PIECES:]

    @pl.when(info[0] == 2)
    def _():
        near_copies = start_pieces(info, pieces, r, near, acc, near_sems)
        copies = start_factor(info, factor, None, lv, acc, sems)
        start_diag(info, head, dt_own, dt_oth, gv, dv, sem)
        subtract(info, acc, before, near, near_copies)
        subtract(info, acc, a, lv, copies)
        wait_diag(gv, dv, sem)
        solve(acc, gv, dv, f)


def finish_kernel(role, info, r, a, head, dt_own, dt_oth, *refs):
    last = role == SIDE - 1
    n_factor = N_PIECES if role == 1 else 1
    factor, refs = refs[:n_factor], refs[n_factor:]
    if last:
        part, earlier, (keep, give, f, acc, lv, gv, dv, sems, sem) = refs[0], refs[1:SIDE], refs[SIDE:]
    else:
        f, acc, lv, gv, dv, sems, sem = refs
    plane, core = info[0], info[1]

    @pl.when(plane == role)
    def _():
        if role == 1:
            copies = start_pieces(info, factor, r, lv, acc, sems)
        else:
            copies = start_factor(info, factor[0], r, lv, acc, sems)
        start_diag(info, head, dt_own, dt_oth, gv, dv, sem)
        subtract(info, acc, a, lv, copies)
        if last:
            acc[...] += part[...].astype(F32)
        wait_diag(gv, dv, sem)
        solve(acc, gv, dv, f)
        if last:
            keep[...] = f[pl.ds(core, 1)][0]
            give[...] = f[pl.ds(1 - core, 1)][0]

    if last:
        for z, done in enumerate(earlier):

            @pl.when(plane == z)
            def _():
                c0 = pltpu.make_async_copy(done.at[core], keep, sems.at[0])
                c1 = pltpu.make_async_copy(done.at[1 - core], give, sems.at[1])
                c0.start()
                c1.start()
                c0.wait()
                c1.wait()


def partial_kernel(info, factor, own, p, acc, lv, sems):
    @pl.when(info[0] == 1)
    def _():
        copies = start_factor(info, factor, None, lv, acc, sems)
        acc[...] = jnp.zeros_like(acc)
        subtract(info, acc, own, lv, copies)
        p[...] = acc[...].astype(BF)


def update_kernel(info, r, to_3, to_2, *refs):
    pieces, (r_out, acc, lv, av, sems, sem) = refs[:N_PIECES], refs[N_PIECES:]

    @pl.when(info[0] >= 2)
    def _():
        for plane, a in ((2, to_2), (3, to_3)):
            pl.when(info[0] == plane)(lambda a=a: pltpu.make_async_copy(a, av, sem).start())
        copies = start_pieces(info, pieces, r, lv, acc, sems)
        pltpu.make_async_copy(to_2, av, sem).wait()
        subtract(info, acc, av, lv, copies)
        out = pltpu.make_async_copy(acc, r_out, sem)
        out.start()
        out.wait()


def mm_t(a, b):
    return lax.dot_general(a, b, (((1,), (1,)), ((), ())), preferred_element_type=F32)


def params(mib=60):
    return pltpu.CompilerParams(vmem_limit_bytes=mib << 20)


def cost(us):
    return pl.CostEstimate(flops=int(us * 1e9), bytes_accessed=1 << 10, transcendentals=0)


def per_device(embeddings, landmarks, factor_rows, diag_inverse):
    tokens, depth = embeddings.shape
    rows = lax.axis_size("rows")
    planes = lax.axis_size("cols") // 2
    here = lax.axis_index("cols")
    plane, core = here // 2, here % 2
    row = lax.axis_index("rows")
    own_rows, blocks, slab = factor_rows.shape
    size = diag_inverse.shape[1]
    lead = landmarks.shape[1]
    n = CHUNKS
    half = tokens // 2
    t = half // n
    scale = 0.5 / math.sqrt(depth)
    per_plane = blocks // planes
    info = jnp.stack([plane, core, row // SIDE, row % SIDE]).astype(jnp.int32)

    def send(x, source, target):
        return lax.ppermute(x, "cols", [(2 * source + k, 2 * target + k) for k in range(2)])

    def swap(x):
        return lax.ppermute(x, "cols", [(c, c ^ 1) for c in range(2 * planes)])

    def fetch(x, by, second):
        pairs = []
        for y in range(SIDE):
            for q in range(SIDE):
                for c in range(2, 2 * planes):
                    along_x = (c % 2 == 0) != second
                    sy, sx = (y, (q + by) % SIDE) if along_x else ((y + by) % SIDE, q)
                    pairs.append(((sy * SIDE + sx) * 2 * planes + c, (y * SIDE + q) * 2 * planes + c))
        return lax.ppermute(x, ("rows", "cols"), pairs)

    def hold(x, *deps):
        return pl.pallas_call(
            hold_kernel,
            in_specs=[ANY] * (1 + len(deps)),
            out_specs=ANY,
            out_shape=jax.ShapeDtypeStruct(x.shape, x.dtype),
            input_output_aliases={0: 0},
            cost_estimate=cost(5),
            name="hold",
        )(x, *deps)

    ft = factor_rows.transpose(1, 2, 0)
    groups = [[r * 2 * planes + 2 * z + k for k in range(2) for r in range(rows)] for z in range(planes)]

    def gather(x):
        everyone = lax.all_gather(x, ("rows", "cols"), axis=0, axis_index_groups=groups)
        return everyone.reshape(2, rows, *x.shape)

    diag = lax.dynamic_slice_in_dim(ft, per_plane * plane, per_plane - 1, 0)
    head = gather(jnp.concatenate([landmarks.T, diag.reshape(-1, own_rows)], axis=0))
    dt_own, dt_oth = diag_inverse, swap(diag_inverse)

    near = ft[:per_plane].reshape(-1, own_rows)
    line = jnp.stack([near] + [fetch(near, by, False) for by in range(1, SIDE)])
    up, down = fetch(line, 1, True), fetch(line, 3, True)
    turn = hold(info, line)
    mid = SIDE // 2
    far = [fetch(up[:mid], 1, True), fetch(down[mid:], 3, True)]
    own = [line, up, down]
    oth = [swap(x) for x in own]
    middle = turn = hold(turn, up, down)
    near = own + far + oth + [swap(x) for x in far]
    turn = hold(turn, *far)

    first = send(ft[per_plane:2 * per_plane], 3, 1)
    other = lax.dynamic_slice_in_dim(ft, per_plane * jnp.maximum(plane - 1, 0), per_plane, 0)
    factor = gather(
        pl.pallas_call(
            pick_kernel,
            in_specs=[SMEM, VMEM, VMEM],
            out_specs=VMEM,
            out_shape=jax.ShapeDtypeStruct((per_plane * slab, own_rows), BF),
            cost_estimate=cost(0),
            name="pick",
        )(middle, first.reshape(-1, own_rows), other.reshape(-1, own_rows))
    )

    chunk_f32 = jax.ShapeDtypeStruct((2, t, own_rows), F32)
    chunk_bf = jax.ShapeDtypeStruct((2, t, own_rows), BF)
    whole_bf = jax.ShapeDtypeStruct((2, half, own_rows), BF)
    diag_scratch = [
        pltpu.VMEM((2, rows, (per_plane - 1) * slab, own_rows), BF),
        pltpu.VMEM((2, 2, size, size), BF),
    ]
    factor_scratch = [
        pltpu.VMEM(chunk_f32.shape, F32),
        pltpu.VMEM((2, rows, per_plane * slab, own_rows), BF),
        pltpu.SemaphoreType.DMA((2 * per_plane + 2,)),
    ]
    r, f0 = [], []
    for q in range(n):
        out = pl.pallas_call(
            functools.partial(scores_kernel, scale, q * t),
            in_specs=[SMEM] + [ANY] * 4,
            out_specs=[VMEM] * 2,
            out_shape=[chunk_f32, chunk_bf],
            scratch_shapes=[pltpu.VMEM((t, depth), BF), pltpu.VMEM((2, rows, lead, own_rows), BF)]
            + diag_scratch
            + [pltpu.SemaphoreType.DMA((5,))],
            compiler_params=params(),
            cost_estimate=cost(5),
            name="scores",
        )(turn, after(embeddings, f0[-1]) if q else embeddings, dt_own, dt_oth, head)
        r.append(out[0])
        f0.append(out[1])
    f0_to_1 = [send(x, 0, 1) for x in f0]
    f0_to_3 = [send(x, 0, 3) for x in f0]
    f0_to_2 = [send(x, 3, 2) for x in f0_to_3]
    r[0] = hold(r[0], f0[-1])

    def finish(role, r, a, more=()):
        last = role == planes - 1
        rows_of = near if role == 1 else [factor]
        one = jax.ShapeDtypeStruct((t, own_rows), BF)
        return pl.pallas_call(
            functools.partial(finish_kernel, role),
            in_specs=[SMEM, ANY, VMEM] + [ANY] * (3 + len(rows_of)) + ([VMEM] + [ANY] * 3 if last else []),
            out_specs=[VMEM] * 2 if last else VMEM,
            out_shape=[one, one] if last else chunk_bf,
            scratch_shapes=([pltpu.VMEM(chunk_bf.shape, BF)] if last else [])
            + factor_scratch[:2]
            + diag_scratch
            + [factor_scratch[2], pltpu.SemaphoreType.DMA((2,))],
            compiler_params=params(),
            cost_estimate=cost(0.8),
            name=f"finish{role}",
        )(info, r, a, head, dt_own, dt_oth, *rows_of, *more)

    def finish_both(r, a, before):
        return pl.pallas_call(
            both_kernel,
            in_specs=[SMEM, ANY, VMEM] + [ANY] * 4 + [VMEM] + [ANY] * N_PIECES,
            out_specs=VMEM,
            out_shape=chunk_bf,
            scratch_shapes=factor_scratch[:2]
            + diag_scratch
            + [factor_scratch[2], pltpu.SemaphoreType.DMA((2,))]
            + factor_scratch[1:],
            compiler_params=params(),
            cost_estimate=cost(0.8),
            name="both2",
        )(info, r, a, head, dt_own, dt_oth, factor, before, *near)

    def partial(own):
        return pl.pallas_call(
            partial_kernel,
            in_specs=[SMEM, ANY, VMEM],
            out_specs=VMEM,
            out_shape=chunk_bf,
            scratch_shapes=factor_scratch,
            compiler_params=params(),
            cost_estimate=cost(0),
            name="partial",
        )(info, factor, own)

    def update(r, to_3, to_2):
        return pl.pallas_call(
            update_kernel,
            in_specs=[SMEM] + [ANY] * (3 + N_PIECES),
            out_specs=ANY,
            out_shape=chunk_f32,
            scratch_shapes=factor_scratch[:2]
            + [pltpu.VMEM(chunk_bf.shape, BF), factor_scratch[2], pltpu.SemaphoreType.DMA],
            compiler_params=params(),
            cost_estimate=cost(0),
            name="update",
        )(info, r, to_3, to_2, *near)

    f1, parts = [], []
    for q in range(n):
        f1.append(finish(1, r[q], after(f0_to_1[q], *f1)))
    f1_to_2 = [send(x, 1, 2) for x in f1]
    r2 = [update(r[0], f0_to_3[0], after(f0_to_2[0], f1[-1]))]
    parts.append(partial(after(f1[0], r2[0])))
    f2 = [finish(2, r2[0], f1_to_2[0])]
    f2.append(finish_both(r[1], f1_to_2[1], after(f0_to_2[1], f2[0])))
    parts.append(partial(after(f1[1], f2[1])))
    r2.append(update(r[1], f0_to_3[1], after(f0_to_2[1], f2[1])))
    parts = [send(x, 1, 3) for x in parts]
    f2_to_3 = [send(x, 2, 3) for x in f2]
    done = []
    for q in range(n):
        a = after(f2_to_3[q], *[x[0] for x in done])
        done.append(finish(3, r2[q], a, (parts[q], f0[q], f1[q], f2[q])))
    keep = [x for x, _ in done]
    got = [swap(x) for _, x in done]
    return jnp.where(core == 0, jnp.concatenate(keep + got, axis=0), jnp.concatenate(got + keep, axis=0))


def solution(mesh):
    in_specs = (P("rows", None), P("cols", "rows"), P("cols", None, "rows"), P("cols", None, None))
    out_specs = P("rows", "cols")
    return jax.shard_map(
        per_device, mesh=mesh, in_specs=in_specs, out_specs=out_specs, check_vma=False
    )
```

```python
import functools
import math

import jax
import jax.numpy as jnp
from jax import lax
from jax.experimental import pallas as pl
from jax.experimental.pallas import tpu as pltpu
from jax.sharding import PartitionSpec as P

CHUNKS = 2
SIDE = 4
LEAD = 64
SLAB = 32
BF = jnp.bfloat16
F32 = jnp.float32
ANY = pl.BlockSpec(memory_space=pl.ANY)
SMEM = pl.BlockSpec(memory_space=pltpu.SMEM)
VMEM = pl.BlockSpec(memory_space=pltpu.VMEM)


def mm(a, b):
    return jnp.dot(a, b, preferred_element_type=F32)


def after(x, *deps):
    return lax.optimization_barrier((x, *deps))[0]


PIECES = ((0, (0, 1, 2, 3)), (1, (0, 1, 2, 3)), (3, (0, 1, 2, 3)), (2, (0, 1)), (2, (2, 3)))
N_PIECES = 2 * len(PIECES)


def piece_places(info):
    core, y, x = info[1], info[2], info[3]
    for which, parity in ((0, core), (1, 1 - core)):
        for i, (e, along) in enumerate(PIECES):
            for j, d in enumerate(along):
                dy, dx = jnp.where(parity == 0, e, d), jnp.where(parity == 0, d, e)
                yield which * len(PIECES) + i, j, parity, ((y + dy) % SIDE) * SIDE + (x + dx) % SIDE


def halves(info):
    return enumerate((info[1], 1 - info[1]))


def start_pieces(info, pieces, r, lv, acc, sems):
    blocks = lv.shape[2] // SLAB
    for i, half in halves(info):
        pltpu.make_async_copy(r.at[half], acc.at[half], sems.at[2 * blocks + i]).start()
    for i, d, parity, place in piece_places(info):
        pltpu.make_async_copy(pieces[i].at[d], lv.at[parity, place], sems.at[i // len(PIECES)]).start()

    def wait(i, half, k):
        if k == 0:
            pltpu.make_async_copy(lv.at[half], lv.at[half], sems.at[i]).wait()
            pltpu.make_async_copy(acc.at[half], acc.at[half], sems.at[2 * blocks + i]).wait()

    return wait


def start_diag(info, head, dt_own, dt_oth, gv, dv, sem):
    core = info[1]
    depth = gv.shape[2]
    pltpu.make_async_copy(head.at[:, :, pl.ds(LEAD, depth)], gv, sem.at[0]).start()
    pltpu.make_async_copy(dt_own, dv.at[core], sem.at[1]).start()
    pltpu.make_async_copy(dt_oth, dv.at[1 - core], sem.at[1]).start()


def wait_diag(gv, dv, sem):
    pltpu.make_async_copy(gv, gv, sem.at[0]).wait()
    pltpu.make_async_copy(dv, dv, sem.at[1]).wait()


def solve(running, diag, dt, f):
    size = dt.shape[-1]

    def column(i):
        return running[i // 2, :, (i % 2) * size:(i % 2 + 1) * size]

    def store(i, value):
        f[i // 2, :, (i % 2) * size:(i % 2 + 1) * size] = value

    def left(i, k):
        block = diag[i // 2, :, k * SLAB:(k + 1) * SLAB, (i % 2) * size:(i % 2 + 1) * size]
        return block.reshape(size, size)

    f0 = mm_t(column(0).astype(BF), dt[0, 0]).astype(BF)
    store(0, f0)
    f1 = mm_t((column(1) - mm(f0, left(1, 0))).astype(BF), dt[0, 1]).astype(BF)
    store(1, f1)
    f2 = mm_t((column(2) - mm(f0, left(2, 0)) - mm(f1, left(2, 1))).astype(BF), dt[1, 0]).astype(BF)
    store(2, f2)
    f3 = column(3) - mm(f0, left(3, 0)) - mm(f1, left(3, 1)) - mm(f2, left(3, 2))
    store(3, mm_t(f3.astype(BF), dt[1, 1]).astype(BF))


def hold_kernel(*refs):
    pass


def pick_kernel(info, first, other, out):
    out[...] = jnp.where(info[0] == 1, first[...], other[...])


def scores_kernel(scale, first, info, embeddings, dt_own, dt_oth, head, out, f, emb, lm, gv, dv, sem):
    plane, core = info[0], info[1]
    tokens = embeddings.shape[0] // 2
    ce = pltpu.make_async_copy(embeddings.at[pl.ds(core * tokens + first, emb.shape[0])], emb, sem.at[4])
    ce.start()
    lead = lm.shape[2]
    copies = [pltpu.make_async_copy(head.at[i, :, pl.ds(0, lead)], lm.at[i], sem.at[2 + i]) for i in range(2)]
    for copy in copies:
        copy.start()
    pl.when(plane == 0)(lambda: start_diag(info, head, dt_own, dt_oth, gv, dv, sem))
    ce.wait()
    for half in range(2):
        copies[half].wait()
        points = lm[half].reshape(emb.shape[1], lm.shape[3])
        out[half] = jnp.exp(mm(emb[...], points) * scale)

    @pl.when(plane == 0)
    def _():
        wait_diag(gv, dv, sem)
        solve(out, gv, dv, f)


def start_factor(info, factor, r, lv, acc, sems):
    blocks = lv.shape[2] // SLAB

    def block(ref, half, k):
        return ref.at[half, :, pl.ds(k * SLAB, SLAB)]

    for i, half in halves(info):
        for k in range(blocks):
            pltpu.make_async_copy(block(factor, half, k), block(lv, half, k), sems.at[i * blocks + k]).start()
            if k == 0 and r is not None:
                pltpu.make_async_copy(r.at[half], acc.at[half], sems.at[2 * blocks + i]).start()

    def wait(i, half, k):
        pltpu.make_async_copy(block(lv, half, k), block(lv, half, k), sems.at[i * blocks + k]).wait()
        if k == 0 and r is not None:
            pltpu.make_async_copy(acc.at[half], acc.at[half], sems.at[2 * blocks + i]).wait()

    return wait


def subtract(info, acc, a, lv, wait):
    size = lv.shape[1] * SLAB

    def body(i, carry):
        half = jnp.where(i == 0, info[1], 1 - info[1])
        for k in range(lv.shape[2] // SLAB):
            wait(i, half, k)
            left = a[k // 2, :, (k % 2) * size:(k % 2 + 1) * size]
            acc[half] = acc[half] - mm(left, lv[half, :, k * SLAB:(k + 1) * SLAB].reshape(size, -1))
        return carry

    lax.fori_loop(0, 2, body, 0)


def both_kernel(info, r, a, head, dt_own, dt_oth, factor, before, *refs):
    pieces, (f, acc, lv, gv, dv, sems, sem, near, near_sems) = refs[:N_PIECES], refs[N_PIECES:]

    @pl.when(info[0] == 2)
    def _():
        near_copies = start_pieces(info, pieces, r, near, acc, near_sems)
        copies = start_factor(info, factor, None, lv, acc, sems)
        start_diag(info, head, dt_own, dt_oth, gv, dv, sem)
        subtract(info, acc, before, near, near_copies)
        subtract(info, acc, a, lv, copies)
        wait_diag(gv, dv, sem)
        solve(acc, gv, dv, f)


def finish_kernel(role, info, r, a, head, dt_own, dt_oth, *refs):
    last = role == SIDE - 1
    n_factor = N_PIECES if role == 1 else 1
    factor, refs = refs[:n_factor], refs[n_factor:]
    if last:
        part, earlier, (keep, give, f, acc, lv, gv, dv, sems, sem, pv, part_sem) = refs[0], refs[1:SIDE], refs[SIDE:]
    else:
        f, acc, lv, gv, dv, sems, sem = refs
    plane, core = info[0], info[1]

    @pl.when(plane == role)
    def _():
        if role == 1:
            copies = start_pieces(info, factor, r, lv, acc, sems)
        else:
            copies = start_factor(info, factor[0], r, lv, acc, sems)
        if last:
            cp = pltpu.make_async_copy(part, pv, part_sem)
            cp.start()
        start_diag(info, head, dt_own, dt_oth, gv, dv, sem)
        subtract(info, acc, a, lv, copies)
        if last:
            cp.wait()
            acc[...] += pv[...].astype(F32)
        wait_diag(gv, dv, sem)
        solve(acc, gv, dv, f)
        if last:
            keep[...] = f[pl.ds(core, 1)][0]
            give[...] = f[pl.ds(1 - core, 1)][0]

    if last:
        for z, done in enumerate(earlier):

            @pl.when(plane == z)
            def _():
                c0 = pltpu.make_async_copy(done.at[core], keep, sems.at[0])
                c1 = pltpu.make_async_copy(done.at[1 - core], give, sems.at[1])
                c0.start()
                c1.start()
                c0.wait()
                c1.wait()


def partial_kernel(info, factor, own, p, acc, lv, sems):
    @pl.when(info[0] == 1)
    def _():
        copies = start_factor(info, factor, None, lv, acc, sems)
        acc[...] = jnp.zeros_like(acc)
        subtract(info, acc, own, lv, copies)
        p[...] = acc[...].astype(BF)


def update_kernel(info, r, to_3, to_2, *refs):
    pieces, (r_out, acc, lv, av, sems, sem) = refs[:N_PIECES], refs[N_PIECES:]

    @pl.when(info[0] >= 2)
    def _():
        for plane, a in ((2, to_2), (3, to_3)):
            pl.when(info[0] == plane)(lambda a=a: pltpu.make_async_copy(a, av, sem).start())
        copies = start_pieces(info, pieces, r, lv, acc, sems)
        pltpu.make_async_copy(to_2, av, sem).wait()
        subtract(info, acc, av, lv, copies)
        out = pltpu.make_async_copy(acc, r_out, sem)
        out.start()
        out.wait()


def mm_t(a, b):
    return lax.dot_general(a, b, (((1,), (1,)), ((), ())), preferred_element_type=F32)


def params(mib=48):
    return pltpu.CompilerParams(vmem_limit_bytes=mib << 20)


def cost(us):
    return pl.CostEstimate(flops=int(us * 1e9), bytes_accessed=1 << 10, transcendentals=0)


def per_device(embeddings, landmarks, factor_rows, diag_inverse):
    tokens, depth = embeddings.shape
    rows = lax.axis_size("rows")
    planes = lax.axis_size("cols") // 2
    here = lax.axis_index("cols")
    plane, core = here // 2, here % 2
    row = lax.axis_index("rows")
    own_rows, blocks, slab = factor_rows.shape
    size = diag_inverse.shape[1]
    lead = landmarks.shape[1]
    n = CHUNKS
    half = tokens // 2
    t = half // n
    scale = 0.5 / math.sqrt(depth)
    per_plane = blocks // planes
    info = jnp.stack([plane, core, row // SIDE, row % SIDE]).astype(jnp.int32)

    def send(x, source, target):
        return lax.ppermute(x, "cols", [(2 * source + k, 2 * target + k) for k in range(2)])

    def swap(x):
        return lax.ppermute(x, "cols", [(c, c ^ 1) for c in range(2 * planes)])

    def fetch(x, by, second):
        pairs = []
        for y in range(SIDE):
            for q in range(SIDE):
                for c in range(2, 2 * planes):
                    along_x = (c % 2 == 0) != second
                    sy, sx = (y, (q + by) % SIDE) if along_x else ((y + by) % SIDE, q)
                    pairs.append(((sy * SIDE + sx) * 2 * planes + c, (y * SIDE + q) * 2 * planes + c))
        return lax.ppermute(x, ("rows", "cols"), pairs)

    def hold(x, *deps):
        return pl.pallas_call(
            hold_kernel,
            in_specs=[ANY] * (1 + len(deps)),
            out_specs=ANY,
            out_shape=jax.ShapeDtypeStruct(x.shape, x.dtype),
            input_output_aliases={0: 0},
            cost_estimate=cost(5),
            name="hold",
        )(x, *deps)

    ft = factor_rows.transpose(1, 2, 0)
    groups = [[r * 2 * planes + 2 * z + k for k in range(2) for r in range(rows)] for z in range(planes)]

    def gather(x):
        everyone = lax.all_gather(x, ("rows", "cols"), axis=0, axis_index_groups=groups)
        return everyone.reshape(2, rows, *x.shape)

    diag = lax.dynamic_slice_in_dim(ft, per_plane * plane, per_plane - 1, 0)
    head = gather(jnp.concatenate([landmarks.T, diag.reshape(-1, own_rows)], axis=0))
    dt_own, dt_oth = diag_inverse, swap(diag_inverse)

    near = ft[:per_plane].reshape(-1, own_rows)
    line = jnp.stack([near] + [fetch(near, by, False) for by in range(1, SIDE)])
    up, down = fetch(line, 1, True), fetch(line, 3, True)
    turn = hold(info, line)
    mid = SIDE // 2
    far = [fetch(up[:mid], 1, True), fetch(down[mid:], 3, True)]
    own = [line, up, down]
    oth = [swap(x) for x in own]
    middle = turn = hold(turn, up, down)
    far_oth = [swap(x) for x in far]
    near = own + far + oth + far_oth
    turn = hold(turn, *far)

    first = send(ft[per_plane:2 * per_plane], 3, 1)
    other = lax.dynamic_slice_in_dim(ft, per_plane * jnp.maximum(plane - 1, 0), per_plane, 0)
    factor = gather(
        pl.pallas_call(
            pick_kernel,
            in_specs=[SMEM, VMEM, VMEM],
            out_specs=VMEM,
            out_shape=jax.ShapeDtypeStruct((per_plane * slab, own_rows), BF),
            cost_estimate=cost(0),
            name="pick",
        )(middle, first.reshape(-1, own_rows), other.reshape(-1, own_rows))
    )

    chunk_f32 = jax.ShapeDtypeStruct((2, t, own_rows), F32)
    chunk_bf = jax.ShapeDtypeStruct((2, t, own_rows), BF)
    whole_bf = jax.ShapeDtypeStruct((2, half, own_rows), BF)
    diag_scratch = [
        pltpu.VMEM((2, rows, (per_plane - 1) * slab, own_rows), BF),
        pltpu.VMEM((2, 2, size, size), BF),
    ]
    factor_scratch = [
        pltpu.VMEM(chunk_f32.shape, F32),
        pltpu.VMEM((2, rows, per_plane * slab, own_rows), BF),
        pltpu.SemaphoreType.DMA((2 * per_plane + 2,)),
    ]
    r, f0 = [], []
    for q in range(n):
        out = pl.pallas_call(
            functools.partial(scores_kernel, scale, q * t),
            in_specs=[SMEM] + [ANY] * 4,
            out_specs=[VMEM] * 2,
            out_shape=[chunk_f32, chunk_bf],
            scratch_shapes=[pltpu.VMEM((t, depth), BF), pltpu.VMEM((2, rows, lead, own_rows), BF)]
            + diag_scratch
            + [pltpu.SemaphoreType.DMA((5,))],
            compiler_params=params(),
            cost_estimate=cost(5),
            name="scores",
        )(turn, after(embeddings, f0[-1], *far_oth) if q else embeddings, dt_own, dt_oth, head)
        r.append(out[0])
        f0.append(out[1])
    f0_to_1 = [send(x, 0, 1) for x in f0]
    f0_to_3 = [send(x, 0, 3) for x in f0]
    f0_to_2 = [send(x, 3, 2) for x in f0_to_3]
    r[0] = hold(r[0], f0[-1])

    def finish(role, r, a, more=()):
        last = role == planes - 1
        rows_of = near if role == 1 else [factor]
        one = jax.ShapeDtypeStruct((t, own_rows), BF)
        return pl.pallas_call(
            functools.partial(finish_kernel, role),
            in_specs=[SMEM, ANY, VMEM] + [ANY] * (3 + len(rows_of)) + ([ANY] * 4 if last else []),
            out_specs=[VMEM] * 2 if last else VMEM,
            out_shape=[one, one] if last else chunk_bf,
            scratch_shapes=([pltpu.VMEM(chunk_bf.shape, BF)] if last else [])
            + factor_scratch[:2]
            + diag_scratch
            + [factor_scratch[2], pltpu.SemaphoreType.DMA((2,))]
            + ([pltpu.VMEM(chunk_bf.shape, BF), pltpu.SemaphoreType.DMA] if last else []),
            compiler_params=params(),
            cost_estimate=cost(0.8),
            name=f"finish{role}",
        )(info, r, a, head, dt_own, dt_oth, *rows_of, *more)

    def finish_both(r, a, before):
        return pl.pallas_call(
            both_kernel,
            in_specs=[SMEM, ANY, VMEM] + [ANY] * 4 + [VMEM] + [ANY] * N_PIECES,
            out_specs=VMEM,
            out_shape=chunk_bf,
            scratch_shapes=factor_scratch[:2]
            + diag_scratch
            + [factor_scratch[2], pltpu.SemaphoreType.DMA((2,))]
            + factor_scratch[1:],
            compiler_params=params(),
            cost_estimate=cost(0.8),
            name="both2",
        )(info, r, a, head, dt_own, dt_oth, factor, before, *near)

    def partial(own):
        return pl.pallas_call(
            partial_kernel,
            in_specs=[SMEM, ANY, VMEM],
            out_specs=VMEM,
            out_shape=chunk_bf,
            scratch_shapes=factor_scratch,
            compiler_params=params(),
            cost_estimate=cost(0),
            name="partial",
        )(info, factor, own)

    def update(r, to_3, to_2):
        return pl.pallas_call(
            update_kernel,
            in_specs=[SMEM] + [ANY] * (3 + N_PIECES),
            out_specs=ANY,
            out_shape=chunk_f32,
            scratch_shapes=factor_scratch[:2]
            + [pltpu.VMEM(chunk_bf.shape, BF), factor_scratch[2], pltpu.SemaphoreType.DMA],
            compiler_params=params(),
            cost_estimate=cost(0),
            name="update",
        )(info, r, to_3, to_2, *near)

    f1, parts = [], []
    for q in range(n):
        f1.append(finish(1, r[q], after(f0_to_1[q], *f1)))
    f1_to_2 = [send(x, 1, 2) for x in f1]
    r2 = [update(r[0], f0_to_3[0], after(f0_to_2[0], f1[-1]))]
    parts.append(partial(after(f1[0], r2[0])))
    f2 = [finish(2, r2[0], f1_to_2[0])]
    f2.append(finish_both(r[1], f1_to_2[1], after(f0_to_2[1], f2[0])))
    parts.append(partial(after(f1[1], f2[1])))
    r2.append(update(r[1], f0_to_3[1], after(f0_to_2[1], f2[1])))
    parts = [send(x, 1, 3) for x in parts]
    f2_to_3 = [send(x, 2, 3) for x in f2]
    done = []
    for q in range(n):
        a = after(f2_to_3[q], *[x[0] for x in done])
        done.append(finish(3, r2[q], a, (parts[q], f0[q], f1[q], f2[q])))
    keep = [x for x, _ in done]
    got = [swap(x) for _, x in done]
    return jnp.where(core == 0, jnp.concatenate(keep + got, axis=0), jnp.concatenate(got + keep, axis=0))


def solution(mesh):
    in_specs = (P("rows", None), P("cols", "rows"), P("cols", None, "rows"), P("cols", None, None))
    out_specs = P("rows", "cols")
    return jax.shard_map(
        per_device, mesh=mesh, in_specs=in_specs, out_specs=out_specs, check_vma=False
    )
```

```python
import functools
import math

import jax
import jax.numpy as jnp
from jax import lax
from jax.experimental import pallas as pl
from jax.experimental.pallas import tpu as pltpu
from jax.sharding import PartitionSpec as P

CHUNKS = 2
SIDE = 4
LEAD = 64
SLAB = 32
BF = jnp.bfloat16
F32 = jnp.float32
ANY = pl.BlockSpec(memory_space=pl.ANY)
SMEM = pl.BlockSpec(memory_space=pltpu.SMEM)
VMEM = pl.BlockSpec(memory_space=pltpu.VMEM)


def mm(a, b):
    return jnp.dot(a, b, preferred_element_type=F32)


def after(x, *deps):
    return lax.optimization_barrier((x, *deps))[0]


PIECES = ((0, (0, 1, 2, 3)), (1, (0, 1, 2, 3)), (3, (0, 1, 2, 3)), (2, (0, 1)), (2, (2, 3)))
N_PIECES = 2 * len(PIECES)


def piece_places(info):
    core, y, x = info[1], info[2], info[3]
    for which, parity in ((0, core), (1, 1 - core)):
        for i, (e, along) in enumerate(PIECES):
            for j, d in enumerate(along):
                dy, dx = jnp.where(parity == 0, e, d), jnp.where(parity == 0, d, e)
                yield which * len(PIECES) + i, j, parity, ((y + dy) % SIDE) * SIDE + (x + dx) % SIDE


def halves(info):
    return enumerate((info[1], 1 - info[1]))


def start_pieces(info, pieces, r, lv, acc, sems):
    blocks = lv.shape[2] // SLAB
    for i, half in halves(info):
        pltpu.make_async_copy(r.at[half], acc.at[half], sems.at[2 * blocks + i]).start()
    for i, d, parity, place in piece_places(info):
        pltpu.make_async_copy(pieces[i].at[d], lv.at[parity, place], sems.at[i // len(PIECES)]).start()

    def wait(i, half, k):
        if k == 0:
            pltpu.make_async_copy(lv.at[half], lv.at[half], sems.at[i]).wait()
            pltpu.make_async_copy(acc.at[half], acc.at[half], sems.at[2 * blocks + i]).wait()

    return wait


def start_diag(info, head, dt_own, dt_oth, gv, dv, sem):
    core = info[1]
    depth = gv.shape[2]
    pltpu.make_async_copy(head.at[:, :, pl.ds(LEAD, depth)], gv, sem.at[0]).start()
    pltpu.make_async_copy(dt_own, dv.at[core], sem.at[1]).start()
    pltpu.make_async_copy(dt_oth, dv.at[1 - core], sem.at[1]).start()


def wait_diag(gv, dv, sem):
    pltpu.make_async_copy(gv, gv, sem.at[0]).wait()
    pltpu.make_async_copy(dv, dv, sem.at[1]).wait()


def solve(running, diag, dt, f):
    size = dt.shape[-1]

    def column(i):
        return running[i // 2, :, (i % 2) * size:(i % 2 + 1) * size]

    def store(i, value):
        f[i // 2, :, (i % 2) * size:(i % 2 + 1) * size] = value

    def left(i, k):
        block = diag[i // 2, :, k * SLAB:(k + 1) * SLAB, (i % 2) * size:(i % 2 + 1) * size]
        return block.reshape(size, size)

    f0 = mm_t(column(0).astype(BF), dt[0, 0]).astype(BF)
    store(0, f0)
    f1 = mm_t((column(1) - mm(f0, left(1, 0))).astype(BF), dt[0, 1]).astype(BF)
    store(1, f1)
    f2 = mm_t((column(2) - mm(f0, left(2, 0)) - mm(f1, left(2, 1))).astype(BF), dt[1, 0]).astype(BF)
    store(2, f2)
    f3 = column(3) - mm(f0, left(3, 0)) - mm(f1, left(3, 1)) - mm(f2, left(3, 2))
    store(3, mm_t(f3.astype(BF), dt[1, 1]).astype(BF))


def hold_kernel(*refs):
    pass


def pick_kernel(info, first, other, out):
    out[...] = jnp.where(info[0] == 1, first[...], other[...])


def scores_kernel(scale, first, info, embeddings, dt_own, dt_oth, head, out, f, emb, lm, gv, dv, sem):
    plane, core = info[0], info[1]
    tokens = embeddings.shape[0] // 2
    ce = pltpu.make_async_copy(embeddings.at[pl.ds(core * tokens + first, emb.shape[0])], emb, sem.at[4])
    ce.start()
    lead = lm.shape[2]
    copies = [pltpu.make_async_copy(head.at[i, :, pl.ds(0, lead)], lm.at[i], sem.at[2 + i]) for i in range(2)]
    for copy in copies:
        copy.start()
    pl.when(plane == 0)(lambda: start_diag(info, head, dt_own, dt_oth, gv, dv, sem))
    ce.wait()
    for half in range(2):
        copies[half].wait()
        points = lm[half].reshape(emb.shape[1], lm.shape[3])
        out[half] = jnp.exp(mm(emb[...], points) * scale)

    @pl.when(plane == 0)
    def _():
        wait_diag(gv, dv, sem)
        solve(out, gv, dv, f)


def start_factor(info, factor, r, lv, acc, sems):
    blocks = lv.shape[2] // SLAB

    def block(ref, half, k):
        return ref.at[half, :, pl.ds(k * SLAB, SLAB)]

    for i, half in halves(info):
        for k in range(blocks):
            pltpu.make_async_copy(block(factor, half, k), block(lv, half, k), sems.at[i * blocks + k]).start()
            if k == 0 and r is not None:
                pltpu.make_async_copy(r.at[half], acc.at[half], sems.at[2 * blocks + i]).start()

    def wait(i, half, k):
        pltpu.make_async_copy(block(lv, half, k), block(lv, half, k), sems.at[i * blocks + k]).wait()
        if k == 0 and r is not None:
            pltpu.make_async_copy(acc.at[half], acc.at[half], sems.at[2 * blocks + i]).wait()

    return wait


def subtract(info, acc, a, lv, wait):
    size = lv.shape[1] * SLAB

    def body(i, carry):
        half = jnp.where(i == 0, info[1], 1 - info[1])
        for k in range(lv.shape[2] // SLAB):
            wait(i, half, k)
            left = a[k // 2, :, (k % 2) * size:(k % 2 + 1) * size]
            acc[half] = acc[half] - mm(left, lv[half, :, k * SLAB:(k + 1) * SLAB].reshape(size, -1))
        return carry

    lax.fori_loop(0, 2, body, 0)


def both_kernel(info, r, a, head, dt_own, dt_oth, factor, before, *refs):
    pieces, (f, acc, lv, gv, dv, sems, sem, near, near_sems) = refs[:N_PIECES], refs[N_PIECES:]

    @pl.when(info[0] == 2)
    def _():
        near_copies = start_pieces(info, pieces, r, near, acc, near_sems)
        copies = start_factor(info, factor, None, lv, acc, sems)
        start_diag(info, head, dt_own, dt_oth, gv, dv, sem)
        subtract(info, acc, before, near, near_copies)
        subtract(info, acc, a, lv, copies)
        wait_diag(gv, dv, sem)
        solve(acc, gv, dv, f)


def finish_kernel(role, info, r, a, head, dt_own, dt_oth, *refs):
    last = role == SIDE - 1
    n_factor = N_PIECES if role == 1 else 1
    factor, refs = refs[:n_factor], refs[n_factor:]
    if last:
        part, earlier, (keep, give, f, acc, lv, gv, dv, sems, sem, pv, part_sem) = refs[0], refs[1:SIDE], refs[SIDE:]
    else:
        f, acc, lv, gv, dv, sems, sem = refs
    plane, core = info[0], info[1]

    @pl.when(plane == role)
    def _():
        if role == 1:
            copies = start_pieces(info, factor, r, lv, acc, sems)
        else:
            copies = start_factor(info, factor[0], r, lv, acc, sems)
        if last:
            cp = pltpu.make_async_copy(part, pv, part_sem)
            cp.start()
        start_diag(info, head, dt_own, dt_oth, gv, dv, sem)
        subtract(info, acc, a, lv, copies)
        if last:
            cp.wait()
            acc[...] += pv[...].astype(F32)
        wait_diag(gv, dv, sem)
        solve(acc, gv, dv, f)
        if last:
            keep[...] = f[pl.ds(core, 1)][0]
            give[...] = f[pl.ds(1 - core, 1)][0]

    if last:
        for z, done in enumerate(earlier):

            @pl.when(plane == z)
            def _():
                c0 = pltpu.make_async_copy(done.at[core], keep, sems.at[0])
                c1 = pltpu.make_async_copy(done.at[1 - core], give, sems.at[1])
                c0.start()
                c1.start()
                c0.wait()
                c1.wait()


def partial_kernel(info, factor, own, p, acc, lv, sems):
    @pl.when(info[0] == 1)
    def _():
        copies = start_factor(info, factor, None, lv, acc, sems)
        acc[...] = jnp.zeros_like(acc)
        subtract(info, acc, own, lv, copies)
        p[...] = acc[...].astype(BF)


def update_kernel(info, r, to_3, to_2, *refs):
    pieces, (r_out, acc, lv, av, sems, sem) = refs[:N_PIECES], refs[N_PIECES:]

    @pl.when(info[0] >= 2)
    def _():
        for plane, a in ((2, to_2), (3, to_3)):
            pl.when(info[0] == plane)(lambda a=a: pltpu.make_async_copy(a, av, sem).start())
        copies = start_pieces(info, pieces, r, lv, acc, sems)
        pltpu.make_async_copy(to_2, av, sem).wait()
        subtract(info, acc, av, lv, copies)
        out = pltpu.make_async_copy(acc, r_out, sem)
        out.start()
        out.wait()


def mm_t(a, b):
    return lax.dot_general(a, b, (((1,), (1,)), ((), ())), preferred_element_type=F32)


def params(mib=48):
    return pltpu.CompilerParams(vmem_limit_bytes=mib << 20)


def cost(us):
    return pl.CostEstimate(flops=int(us * 1e9), bytes_accessed=1 << 10, transcendentals=0)


def per_device(embeddings, landmarks, factor_rows, diag_inverse):
    tokens, depth = embeddings.shape
    rows = lax.axis_size("rows")
    planes = lax.axis_size("cols") // 2
    here = lax.axis_index("cols")
    plane, core = here // 2, here % 2
    row = lax.axis_index("rows")
    own_rows, blocks, slab = factor_rows.shape
    size = diag_inverse.shape[1]
    lead = landmarks.shape[1]
    n = CHUNKS
    half = tokens // 2
    t = half // n
    scale = 0.5 / math.sqrt(depth)
    per_plane = blocks // planes
    info = jnp.stack([plane, core, row // SIDE, row % SIDE]).astype(jnp.int32)

    def send(x, source, target):
        return lax.ppermute(x, "cols", [(2 * source + k, 2 * target + k) for k in range(2)])

    def swap(x):
        return lax.ppermute(x, "cols", [(c, c ^ 1) for c in range(2 * planes)])

    def fetch(x, by, second):
        pairs = []
        for y in range(SIDE):
            for q in range(SIDE):
                for c in range(2, 2 * planes):
                    along_x = (c % 2 == 0) != second
                    sy, sx = (y, (q + by) % SIDE) if along_x else ((y + by) % SIDE, q)
                    pairs.append(((sy * SIDE + sx) * 2 * planes + c, (y * SIDE + q) * 2 * planes + c))
        return lax.ppermute(x, ("rows", "cols"), pairs)

    def hold(x, *deps):
        return pl.pallas_call(
            hold_kernel,
            in_specs=[ANY] * (1 + len(deps)),
            out_specs=ANY,
            out_shape=jax.ShapeDtypeStruct(x.shape, x.dtype),
            input_output_aliases={0: 0},
            cost_estimate=cost(5),
            name="hold",
        )(x, *deps)

    ft = factor_rows.transpose(1, 2, 0)
    groups = [[r * 2 * planes + 2 * z + k for k in range(2) for r in range(rows)] for z in range(planes)]

    def gather(x):
        everyone = lax.all_gather(x, ("rows", "cols"), axis=0, axis_index_groups=groups)
        return everyone.reshape(2, rows, *x.shape)

    diag = lax.dynamic_slice_in_dim(ft, per_plane * plane, per_plane - 1, 0)
    head = gather(jnp.concatenate([landmarks.T, diag.reshape(-1, own_rows)], axis=0))
    dt_own, dt_oth = diag_inverse, swap(diag_inverse)

    near = ft[:per_plane].reshape(-1, own_rows)
    line = jnp.stack([near] + [fetch(near, by, False) for by in range(1, SIDE)])
    up, down = fetch(line, 1, True), fetch(line, 3, True)
    turn = hold(info, line)
    mid = SIDE // 2
    far = [fetch(up[:mid], 1, True), fetch(down[mid:], 3, True)]
    own = [line, up, down]
    oth = [swap(x) for x in own]
    middle = turn = hold(turn, up, down)
    far_oth = [swap(x) for x in far]
    near = own + far + oth + far_oth
    turn = hold(turn, *far)

    first = send(ft[per_plane:2 * per_plane], 3, 1)
    other = lax.dynamic_slice_in_dim(ft, per_plane * jnp.maximum(plane - 1, 0), per_plane, 0)
    factor = gather(
        pl.pallas_call(
            pick_kernel,
            in_specs=[SMEM, VMEM, VMEM],
            out_specs=VMEM,
            out_shape=jax.ShapeDtypeStruct((per_plane * slab, own_rows), BF),
            cost_estimate=cost(0),
            name="pick",
        )(middle, first.reshape(-1, own_rows), other.reshape(-1, own_rows))
    )

    chunk_f32 = jax.ShapeDtypeStruct((2, t, own_rows), F32)
    chunk_bf = jax.ShapeDtypeStruct((2, t, own_rows), BF)
    whole_bf = jax.ShapeDtypeStruct((2, half, own_rows), BF)
    diag_scratch = [
        pltpu.VMEM((2, rows, (per_plane - 1) * slab, own_rows), BF),
        pltpu.VMEM((2, 2, size, size), BF),
    ]
    factor_scratch = [
        pltpu.VMEM(chunk_f32.shape, F32),
        pltpu.VMEM((2, rows, per_plane * slab, own_rows), BF),
        pltpu.SemaphoreType.DMA((2 * per_plane + 2,)),
    ]
    r, f0 = [], []
    for q in range(n):
        out = pl.pallas_call(
            functools.partial(scores_kernel, scale, q * t),
            in_specs=[SMEM] + [ANY] * 4,
            out_specs=[VMEM] * 2,
            out_shape=[chunk_f32, chunk_bf],
            scratch_shapes=[pltpu.VMEM((t, depth), BF), pltpu.VMEM((2, rows, lead, own_rows), BF)]
            + diag_scratch
            + [pltpu.SemaphoreType.DMA((5,))],
            compiler_params=params(),
            cost_estimate=cost(5),
            name="scores",
        )(turn, after(embeddings, f0[-1], *far_oth) if q else embeddings, dt_own, dt_oth, head)
        r.append(out[0])
        f0.append(out[1])
    f0_to_1 = [send(x, 0, 1) for x in f0]
    f0_to_3 = [send(x, 0, 3) for x in f0]
    f0_to_2 = [send(x, 3, 2) for x in f0_to_3]
    r[0] = hold(r[0], f0[-1])

    def finish(role, r, a, more=()):
        last = role == planes - 1
        rows_of = near if role == 1 else [factor]
        one = jax.ShapeDtypeStruct((t, own_rows), BF)
        return pl.pallas_call(
            functools.partial(finish_kernel, role),
            in_specs=[SMEM, ANY, VMEM] + [ANY] * (3 + len(rows_of)) + ([ANY] * 4 if last else []),
            out_specs=[VMEM] * 2 if last else VMEM,
            out_shape=[one, one] if last else chunk_bf,
            scratch_shapes=([pltpu.VMEM(chunk_bf.shape, BF)] if last else [])
            + factor_scratch[:2]
            + diag_scratch
            + [factor_scratch[2], pltpu.SemaphoreType.DMA((2,))]
            + ([pltpu.VMEM(chunk_bf.shape, BF), pltpu.SemaphoreType.DMA] if last else []),
            compiler_params=params(),
            cost_estimate=cost(0.8),
            name=f"finish{role}",
        )(info, r, a, head, dt_own, dt_oth, *rows_of, *more)

    def finish_both(r, a, before):
        return pl.pallas_call(
            both_kernel,
            in_specs=[SMEM, ANY, VMEM] + [ANY] * 4 + [VMEM] + [ANY] * N_PIECES,
            out_specs=VMEM,
            out_shape=chunk_bf,
            scratch_shapes=factor_scratch[:2]
            + diag_scratch
            + [factor_scratch[2], pltpu.SemaphoreType.DMA((2,))]
            + factor_scratch[1:],
            compiler_params=params(),
            cost_estimate=cost(0.8),
            name="both2",
        )(info, r, a, head, dt_own, dt_oth, factor, before, *near)

    def partial(own):
        return pl.pallas_call(
            partial_kernel,
            in_specs=[SMEM, ANY, VMEM],
            out_specs=VMEM,
            out_shape=chunk_bf,
            scratch_shapes=factor_scratch,
            compiler_params=params(),
            cost_estimate=cost(0),
            name="partial",
        )(info, factor, own)

    def update(r, to_3, to_2):
        return pl.pallas_call(
            update_kernel,
            in_specs=[SMEM] + [ANY] * (3 + N_PIECES),
            out_specs=ANY,
            out_shape=chunk_f32,
            scratch_shapes=factor_scratch[:2]
            + [pltpu.VMEM(chunk_bf.shape, BF), factor_scratch[2], pltpu.SemaphoreType.DMA],
            compiler_params=params(),
            cost_estimate=cost(0),
            name="update",
        )(info, r, to_3, to_2, *near)

    f1, parts = [], []
    for q in range(n):
        f1.append(finish(1, r[q], after(f0_to_1[q], *f1)))
    f1_to_2 = [send(x, 1, 2) for x in f1]
    r2 = [update(r[0], f0_to_3[0], after(f0_to_2[0], f1[-1]))]
    parts.append(partial(after(f1[0], r2[0])))
    f2 = [finish(2, r2[0], f1_to_2[0])]
    f2.append(finish_both(r[1], f1_to_2[1], after(f0_to_2[1], f2[0])))
    parts.append(partial(after(f1[1], f2[1])))
    r2.append(update(r[1], f0_to_3[1], after(f0_to_2[1], f2[1])))
    parts = [send(x, 1, 3) for x in parts]
    f2_to_3 = [send(x, 2, 3) for x in f2]
    done = []
    for q in range(n):
        a = after(f2_to_3[q], *[x[0] for x in done])
        done.append(finish(3, r2[q], a, (parts[q], f0[q], f1[q], f2[q])))
    keep = [x for x, _ in done]
    got = [swap(x) for _, x in done]
    ahead = [jnp.where(core == 0, x, y) for x, y in zip(keep, got)]
    behind = [jnp.where(core == 0, y, x) for x, y in zip(keep, got)]
    return jnp.concatenate(ahead + behind, axis=0)


def solution(mesh):
    in_specs = (P("rows", None), P("cols", "rows"), P("cols", None, "rows"), P("cols", None, None))
    out_specs = P("rows", "cols")
    return jax.shard_map(
        per_device, mesh=mesh, in_specs=in_specs, out_specs=out_specs, check_vma=False
    )
```
